128 devices in a mesh: lat: 8 (over x, z_lo), lon: 8 (over y, core), tp: 2 (over z_hi).
Axes of the slice: x: 4, y: 4, z: 4 (z_hi: 2, z_lo: 2; z = z_hi * 2 + z_lo), core: 2. Of those that a mesh axis runs over, the one named last changes fastest.
Arguments:
- tokens: bfloat16 [4, 48, 192, 1024], P(None, 'lat', 'lon', 'tp'), may hold values from -6 to 6
- w_qkv: bfloat16 [1024, 3, 1024], P(None, None, 'tp'), may hold values from -0.1875 to 0.1875
- w_proj: bfloat16 [1024, 1024], P(None, 'tp'), may hold values from -0.1875 to 0.1875
- bias_table: float32 [759, 16], P(None, 'tp'), may hold values from -4 to 4
- bias_index: int32 [144, 144], replicated, may hold values from 0 to 758
- regions: int32 [4, 48, 192], P(None, 'lat', 'lon'), may hold values from 0 to 8, as said below
- out_grad: bfloat16 [4, 48, 192, 1024], P(None, 'lat', 'lon', 'tp'), may hold values from -6 to 6
Outputs:
- grad_tokens: bfloat16 [4, 48, 192, 1024], P(None, 'lat', 'lon', 'tp')
- qkv_grad: float32 [1024, 3, 1024], P(('lat', 'lon'), None, 'tp')
- proj_grad: float32 [1024, 1024], P(('lat', 'lon'), 'tp')
The draws below stay inside these ranges and needn't reach their ends.
Inputs may be any that keep to these rules, and one draw needn't show every extreme that they name: `regions`: region ids in the shifted frame follow the shifted-window layout: levels split into the blocks [0, 2), [2, 3), [3, 4) and latitude rows into [0, 42), [42, 45), [45, 48); the id is constant on each of the nine combinations of a level block and a row block, for all longitudes; every id is 0 or 8, and ids of different blocks may coincide. `bias_index`: entries of bias_table's first dimension.
All inputs are finite; a program needn't handle non-finite values.
Results may differ from the reference program's by a relative error of at most 0.014.
Values may be sent and summed in bfloat16 or wider, within the bound.
A program may use at most 128 MiB of HBM per device.

```python
import jax
import jax.numpy as jnp
from jax import lax

D = 1024
H = 16
HD = 64
WL = 2
WA = 6
WB = 12
LEV = 4
WT = 144
NBIAS = 759
NLAT = 48
NLON = 192
N_TP = 2


def draw_regions(key, part):
    key = jax.random.fold_in(key, 7)
    level_pos = jnp.arange(LEV, dtype=jnp.int32)
    row_pos = jnp.arange(NLAT, dtype=jnp.int32)
    level_block = (level_pos >= LEV - WL).astype(jnp.int32) + (level_pos >= LEV - WL // 2).astype(jnp.int32)
    row_block = (row_pos >= NLAT - WA).astype(jnp.int32) + (row_pos >= NLAT - WA // 2).astype(jnp.int32)
    table = 8 * jax.random.randint(key, (3, 3), 0, 2, dtype=jnp.int32)
    table = table.at[0, 0].set(0)
    picked = table[level_block[:, None], row_block[None, :]]
    return jnp.broadcast_to(picked[:, :, None], (LEV, NLAT, NLON)).astype(jnp.int32)


def place_ends(result, rng, low, top_value):
    dims = result.shape
    spot = [jax.random.randint(jax.random.fold_in(rng, axis), (), 0, dims[axis]) for axis in range(len(dims))]
    result = result.at[tuple(spot)].set(low)
    longest = dims.index(max(dims))
    spot[longest] = (spot[longest] + 1) % dims[longest]
    return result.at[tuple(spot)].set(top_value)


def raised(array, key, source, target, parts, factor):
    owner, partner = [(jnp.arange(array.shape[position]) // (array.shape[position] // parts)).reshape([-1 if axis == position else 1 for axis in range(array.ndim)]) for position in (source, target)]
    chosen = jax.random.permutation(key, parts)[partner]
    strong = (owner == chosen) | (owner == (partner + parts // 2) % parts)
    return jnp.where(strong, factor * array, array)


def block_levels(own_key, shape, pieces, smallest, largest):
    level, own = 1.0, jax.random.fold_in(own_key, 6)
    for position, shards_of in pieces:
        heights = jnp.exp(jax.random.uniform(jax.random.fold_in(own, position), (shards_of,), jnp.float32, smallest / len(pieces), largest / len(pieces)))
        level = level * jnp.repeat(heights, shape[position] // shards_of).reshape([-1 if axis == position else 1 for axis in range(len(shape))])
    return level


def noise(rng, dims, scale, limit, split=(), kind=jnp.bfloat16):
    drawn = jax.random.normal(rng, dims, jnp.float32) * scale
    if len(split) > 0:
        drawn = block_levels(rng, dims, split, -0.22, 0.18) * drawn
    return jnp.clip(drawn, min=-limit, max=limit).astype(kind)


def bell_draw_with(key, extent, deviation, most, shards, heavy, held_as=jnp.bfloat16):
    drawn = deviation * jax.random.normal(key, extent, jnp.float32)
    if shards:
        drawn = drawn * block_levels(key, extent, shards, -0.22, 0.18)
    return jnp.clip(raised(drawn, jax.random.fold_in(key, 3), *heavy), -most, most).astype(held_as)


def setup_inputs(seed: int = 0) -> dict:
    key_list = jax.random.split(jax.random.key(seed), 8)
    return {
        "tokens": noise(key_list[0], (LEV, NLAT, NLON, D), 1.0, 6.0, ((1, 8), (2, 8), (3, 2))),
        "w_qkv": noise(key_list[1], (D, 3, D), D ** -0.5, 0.1875, ((2, 2),)),
        "w_proj": noise(key_list[2], (D, D), D ** -0.5, 0.1875, ((1, 2),)),
        "bias_table": noise(key_list[3], (NBIAS, H), 1.0, 4.0, ((1, 2),), jnp.float32),
        "bias_index": place_ends(jax.random.randint(key_list[4], (WT, WT), 0, NBIAS), jax.random.fold_in(key_list[4], 1), 0, NBIAS - 1).astype(jnp.int32),
        "regions": draw_regions(jax.random.fold_in(key_list[7], 71), 0),
        "out_grad": bell_draw_with(key_list[6], (LEV, NLAT, NLON, D), 1.0, 6.0, ((1, 8), (2, 8), (3, 2)), (1, 3, 8, 2.0)),
    }


def to_windows(values):
    levels, row_count, col_count, feat_count = values.shape
    values = values.reshape(levels // WL, WL, row_count // WA, WA, col_count // WB, WB, feat_count)
    values = values.transpose(0, 2, 4, 1, 3, 5, 6)
    return values.reshape(-1, WL * WA * WB, feat_count)

def from_windows(values, levels, row_count, col_count):
    feat_count = values.shape[-1]
    values = values.reshape(levels // WL, row_count // WA, col_count // WB, WL, WA, WB, feat_count)
    values = values.transpose(0, 3, 1, 4, 2, 5, 6)
    return values.reshape(levels, row_count, col_count, feat_count)

def attention_grads(shifted_in, shifted_grad, regions, w_qkv, w_proj, bias_table, bias_index):
    levels, row_count, col_count, model_width = shifted_in.shape
    inner_width = w_qkv.shape[2]
    head_count = inner_width // HD
    cell_count = levels * row_count * col_count
    scale = HD ** (-0.5)
    flat_in = shifted_in.reshape(cell_count, model_width).astype(jnp.float32)
    center = lax.optimization_barrier(jnp.mean(flat_in, axis=1, keepdims=True))
    spread = lax.optimization_barrier(jnp.mean(jnp.square(flat_in - center), axis=1, keepdims=True))
    inv_std = lax.rsqrt(spread + 1e-05)
    normed = (flat_in - center) * inv_std
    normed_bf = normed.astype(jnp.bfloat16)
    qkv_flat = jnp.dot(normed_bf, w_qkv.reshape(model_width, 3 * inner_width), preferred_element_type=jnp.float32).astype(jnp.bfloat16)
    qkv_win = to_windows(qkv_flat.reshape(levels, row_count, col_count, 3 * inner_width))
    count_win, window = (qkv_win.shape[0], qkv_win.shape[1])
    split_heads = qkv_win.reshape(count_win, window, 3, head_count, HD).transpose(2, 0, 3, 1, 4)
    queries, key_part, value_part = (split_heads[0], split_heads[1], split_heads[2])
    table_bias = jnp.take(bias_table, bias_index, axis=0).transpose(2, 0, 1)
    region_win = to_windows(regions[..., None])[..., 0]
    allowed = (region_win[:, :, None] == region_win[:, None, :])[:, None]
    scores = jnp.einsum('whid,whjd->whij', queries.astype(jnp.float32), key_part.astype(jnp.float32)) * scale + table_bias
    exp_scores = jnp.where(allowed, jnp.exp(scores), 0.0)
    attn_probs = exp_scores / lax.optimization_barrier(jnp.sum(exp_scores, axis=-1, keepdims=True))
    probs_bf = attn_probs.astype(jnp.bfloat16)
    attended = jnp.einsum('whij,whjd->whid', probs_bf.astype(jnp.float32), value_part.astype(jnp.float32)).astype(jnp.bfloat16)
    attended_flat = from_windows(attended.transpose(0, 2, 1, 3).reshape(count_win, window, inner_width), levels, row_count, col_count).reshape(cell_count, inner_width)
    grad_flat = shifted_grad.reshape(cell_count, model_width)
    grad_attn = jnp.dot(grad_flat, w_proj, preferred_element_type=jnp.float32).astype(jnp.bfloat16)
    grad_win = to_windows(grad_attn.reshape(levels, row_count, col_count, inner_width))
    grad_win = grad_win.reshape(count_win, window, head_count, HD).transpose(0, 2, 1, 3)
    grad_probs = jnp.einsum('whid,whjd->whij', grad_win.astype(jnp.float32), value_part.astype(jnp.float32))
    grad_value = jnp.einsum('whij,whid->whjd', probs_bf.astype(jnp.float32), grad_win.astype(jnp.float32)).astype(jnp.bfloat16)
    grad_scores = (attn_probs * (grad_probs - lax.optimization_barrier(jnp.sum(attn_probs * grad_probs, axis=-1, keepdims=True))) * scale).astype(jnp.bfloat16)
    grad_query = jnp.einsum('whij,whjd->whid', grad_scores.astype(jnp.float32), key_part.astype(jnp.float32)).astype(jnp.bfloat16)
    grad_key = jnp.einsum('whij,whid->whjd', grad_scores.astype(jnp.float32), queries.astype(jnp.float32)).astype(jnp.bfloat16)
    stacked = jnp.stack([grad_query, grad_key, grad_value], axis=2)
    stacked = stacked.transpose(0, 3, 2, 1, 4).reshape(count_win, window, 3 * inner_width)
    grad_qkv = from_windows(stacked, levels, row_count, col_count).reshape(cell_count, 3 * inner_width)
    return (normed, inv_std, normed_bf, grad_qkv, grad_flat, attended_flat)

def reference(tokens, w_qkv, w_proj, bias_table, bias_index, regions, out_grad):
    forward = (-(WL // 2), -(WA // 2), -(WB // 2))
    backward = (WL // 2, WA // 2, WB // 2)
    shifted_in = jnp.roll(tokens, forward, (0, 1, 2))
    shifted_grad = jnp.roll(out_grad, forward, (0, 1, 2))
    band_count = NLAT // WA
    in_bands = shifted_in.reshape(LEV, band_count, WA, NLON, D).transpose(1, 0, 2, 3, 4)
    grad_bands = shifted_grad.reshape(LEV, band_count, WA, NLON, D).transpose(1, 0, 2, 3, 4)
    region_bands = regions.reshape(LEV, band_count, WA, NLON).transpose(1, 0, 2, 3)
    group_width = D // N_TP
    contract = (((0,), (0,)), ((), ()))

    def band_step(carry, inputs):
        band_in, band_grad, band_regions = inputs
        normed, inv_std, normed_bf, grad_qkv, grad_flat, attended_flat = attention_grads(band_in, band_grad, band_regions, w_qkv, w_proj, bias_table, bias_index)
        cell_count = normed.shape[0]
        grad_three = grad_qkv.reshape(cell_count, 3, D)
        grad_normed = jnp.zeros((cell_count, D), jnp.float32)
        for group in range(N_TP):
            lower = group * group_width
            part_left = grad_three[:, :, lower:lower + group_width].reshape(cell_count, 3 * group_width)
            part_right = w_qkv[:, :, lower:lower + group_width].reshape(D, 3 * group_width)
            part_value = jnp.dot(part_left, part_right.T, preferred_element_type=jnp.float32).astype(jnp.bfloat16)
            grad_normed = grad_normed + lax.optimization_barrier(part_value).astype(jnp.float32)
        mean_grad = lax.optimization_barrier(jnp.mean(grad_normed, axis=1, keepdims=True))
        mean_cross = lax.optimization_barrier(jnp.mean(grad_normed * normed, axis=1, keepdims=True))
        grad_band = (inv_std * (grad_normed - mean_grad - normed * mean_cross)).astype(jnp.bfloat16)
        qkv_acc = carry[0] + lax.dot_general(normed_bf, grad_qkv, contract, preferred_element_type=jnp.float32)
        proj_acc = carry[1] + lax.dot_general(grad_flat, attended_flat, contract, preferred_element_type=jnp.float32)
        return ((qkv_acc, proj_acc), grad_band.reshape(LEV, WA, NLON, D))
    start_carry = (jnp.zeros((D, 3 * D), jnp.float32), jnp.zeros((D, D), jnp.float32))
    (qkv_acc, proj_acc), grad_out_bands = lax.scan(band_step, start_carry, (in_bands, grad_bands, region_bands))
    grad_shifted = grad_out_bands.transpose(1, 0, 2, 3, 4).reshape(LEV, NLAT, NLON, D)
    grad_tokens = jnp.roll(grad_shifted, backward, (0, 1, 2))
    return (grad_tokens, qkv_acc.reshape(D, 3, D), proj_acc)
```

```python
import functools

import jax
import jax.numpy as jnp
import numpy as np
from jax import lax
from jax.experimental import pallas as pl
from jax.experimental.pallas import tpu as pltpu
from jax.sharding import PartitionSpec as P

HD = 64
WT = 144
BIG = 112
SMALL = 48
PIECE = BIG + SMALL
MESH = pl.DeviceIdType.MESH
BF = jnp.bfloat16
F32 = jnp.float32
FAR = -1e30


def permutations():
    pack = np.zeros((2, PIECE, 288), np.float32)
    place = np.zeros((288, 2 * PIECE), np.float32)
    for di in range(2):
        for lv in range(2):
            for row in range(3):
                local = row + (3 if di == 0 else 0)
                for col in range(24):
                    if col >= 6:
                        spot = lv * 54 + row * 18 + col - 6
                    else:
                        spot = BIG + lv * 18 + row * 6 + col
                    pack[di, spot, lv * 144 + local * 24 + col] = 1
                    shifted = (col - 6) % 24
                    cell = (shifted // 12) * 144 + lv * 72 + (row + 3 * di) * 12 + shifted % 12
                    place[cell, di * PIECE + spot] = 1
    return pack, place


PACK, PLACE = permutations()


def position():
    lat, lon, tp = lax.axis_index("lat"), lax.axis_index("lon"), lax.axis_index("tp")
    return lat, lon, tp


def device(lat, lon, tp):
    return {"lat": lat, "lon": lon, "tp": tp}


def neighbours():
    lat, lon, tp = position()
    x, zl, y, core = lat // 2, lat % 2, lon // 2, lon % 2
    sibling = device(lat, y * 2 + 1 - core, tp)
    along_x = [device(((x + d) % 4) * 2 + zl, lon, tp) for d in (1, 2, 3)]
    along_y = [device(lat, ((y + d) % 4) * 2 + core, tp) for d in (1, 2, 3)]
    along_z = device(x * 2 + 1 - zl, lon, tp)
    partner = device(lat, lon, 1 - tp)
    return x, zl, y, core, sibling, along_x, along_y, along_z, partner


def enter(targets):
    barrier = pltpu.get_barrier_semaphore()
    for target in targets:
        pl.semaphore_signal(barrier, inc=1, device_id=target, device_id_type=MESH)
    pl.semaphore_wait(barrier, len(targets))


def piece_ends(sign):
    lat, lon, tp = position()
    ends = []
    for di in range(2):
        for dj in range(2):
            for other in range(2):
                if di == 0 and dj == 0 and other == 0:
                    continue
                to_tp = 1 - tp if other else tp
                ends.append((di, dj, to_tp, device((lat + sign * di + 8) % 8, (lon + sign * dj + 8) % 8, to_tp)))
    return ends


def send(src, dst, send_sem, recv_sem, target):
    copy = pltpu.make_async_remote_copy(
        src_ref=src, dst_ref=dst, send_sem=send_sem, recv_sem=recv_sem, device_id=target, device_id_type=MESH
    )
    copy.start()
    return copy


def bring_kernel(tok_ref, grad_ref, pack_ref, wq_ref, wp_ref, table_ref, held_ref, other_ref, tables_ref,
                 packed, piece_send, piece_recv, w_send, w_recv, local_sem):
    lat, lon, tp = position()
    x, zl, y, core, sibling, along_x, along_y, along_z, partner = neighbours()
    ends = piece_ends(-1)
    sources = piece_ends(1)
    enter([e[3] for e in sources] + [sibling, along_z, partner] + along_x + along_y)

    mine = ((x * 2 + zl) * 4 + y) * 2 + core
    first = [
        send(wq_ref.at[:, mine], other_ref.at[0:3, x, zl, y, core], w_send.at[0], w_recv.at[0], partner),
        send(wp_ref.at[mine], other_ref.at[3, x, zl, y, core], w_send.at[1], w_recv.at[1], partner),
    ]
    tables_ref[0] = jnp.zeros((8, 768), F32)
    tables_ref[0, :, 0:759] = table_ref[...]
    table_copy = send(tables_ref.at[0], tables_ref.at[1], w_send.at[2], w_recv.at[2], partner)

    for half in range(2):
        for di in range(2):
            for which, ref in enumerate((tok_ref, grad_ref)):
                if half == 0:
                    cells = ref[144:432, :]
                else:
                    cells = jnp.concatenate([ref[432:576, :], ref[0:144, :]], axis=0)
                moved = jnp.dot(pack_ref[di], cells, preferred_element_type=F32).astype(BF)
                packed[half, di, which * BIG:(which + 1) * BIG, :] = moved[0:BIG]
                base = 2 * BIG + which * SMALL
                packed[half, di, base:base + SMALL, :] = moved[BIG:PIECE]

    spans = (pl.ds(0, 2 * BIG), pl.ds(2 * BIG, 2 * SMALL))
    pieces = []
    for n, (di, dj, to_tp, target) in enumerate(ends):
        pieces.append(send(packed.at[to_tp, di, spans[dj]], held_ref.at[tp, di, spans[dj]],
                           piece_send.at[n], piece_recv.at[n], target))
    own = pltpu.make_async_copy(packed.at[tp, 0, spans[0]], held_ref.at[tp, 0, spans[0]], local_sem)
    own.start()

    for copy in first:
        copy.wait()
    second = send(other_ref.at[:, x, zl, y, core], other_ref.at[:, x, zl, y, core], w_send.at[3], w_recv.at[3], along_z)
    second.wait()
    third = []
    for d in range(3):
        third.append(send(other_ref.at[0:2, x, :, y, core], other_ref.at[0:2, x, :, y, core],
                          w_send.at[4 + d], w_recv.at[4 + d], along_x[d]))
        third.append(send(other_ref.at[2:4, x, :, y, core], other_ref.at[2:4, x, :, y, core],
                          w_send.at[7 + d], w_recv.at[7 + d], along_y[d]))
    for copy in third:
        copy.wait()
    fourth = []
    for d in range(3):
        fourth.append(send(other_ref.at[0:2, :, :, y, core], other_ref.at[0:2, :, :, y, core],
                           w_send.at[10 + d], w_recv.at[10 + d], along_y[d]))
        fourth.append(send(other_ref.at[2:4, x, :, :, core], other_ref.at[2:4, x, :, :, core],
                           w_send.at[13 + d], w_recv.at[13 + d], along_x[d]))
    for copy in fourth:
        copy.wait()
    fifth = send(other_ref.at[:, :, :, :, core], other_ref.at[:, :, :, :, core], w_send.at[16], w_recv.at[16], sibling)
    fifth.wait()
    own.wait()
    table_copy.wait()
    for copy in pieces:
        copy.wait()


def bias_kernel(tables_ref, index_ref, regions_ref, bias_ref):
    tp = lax.axis_index("tp")
    rows = lax.broadcasted_iota(jnp.int32, (WT, WT), 0) // 12
    cols = lax.broadcasted_iota(jnp.int32, (WT, WT), 1) // 12
    left = jnp.zeros((WT, WT), jnp.int32)
    right = jnp.zeros((WT, WT), jnp.int32)
    for lv in range(2):
        for row in range(6):
            value = regions_ref[2 * tp + lv, row, 0]
            left = jnp.where(rows == lv * 6 + row, value, left)
            right = jnp.where(cols == lv * 6 + row, value, right)
    blocked = jnp.where(left == right, 0.0, FAR).astype(F32)

    blocks = []
    for s in range(2):
        table = tables_ref[s]
        top = table.astype(BF).astype(F32)
        rest = table - top
        mid = rest.astype(BF).astype(F32)
        low = rest - mid
        for part in (top, mid, low):
            for g in range(3):
                blocks.append(part[:, g * 256:(g + 1) * 256])
    matrix = jnp.concatenate(blocks, axis=0).astype(BF)
    depth = lax.broadcasted_iota(jnp.int32, (256, WT), 0)

    def some_rows(step, carry):
        found = ([], [])
        index = index_ref[pl.ds(pl.multiple_of(step * 8, 8), 8), :]
        for r in range(8):
            row = index[r:r + 1, :]
            low_part, high_part = row & 255, row >> 8
            hot = jnp.where(depth == low_part, 1.0, 0.0).astype(BF)
            picked = jnp.dot(matrix, hot, preferred_element_type=F32)
            for s in range(2):
                total = jnp.zeros((8, WT), F32)
                for g in range(3):
                    base = s * 72 + g * 8
                    value = picked[base:base + 8] + picked[base + 24:base + 32] + picked[base + 48:base + 56]
                    total = jnp.where(high_part == g, value, total)
                found[s].append(total)
        for s in range(2):
            stacked = jnp.stack(found[s], axis=0)
            bias_ref[s * 8:(s + 1) * 8, pl.ds(pl.multiple_of(step * 8, 8), 8), :] = jnp.transpose(stacked, (1, 0, 2))
        return carry

    lax.fori_loop(0, WT // 8, some_rows, 0)
    for h in range(16):
        bias_ref[h] = bias_ref[h] + blocked


def work_kernel(held_ref, place_ref, placet_ref, wq_ref, wp_ref, other_ref, bias_ref, sums_ref, back_ref,
                normed, normed_bf, grads, normed_t, grads_t, inv, parts, dparts, att, dx):
    def gather(which):
        halves = []
        for t in range(2):
            rows = []
            for di in range(2):
                rows.append(held_ref[t, di, which * BIG:(which + 1) * BIG, :])
                base = 2 * BIG + which * SMALL
                rows.append(held_ref[t, di, base:base + SMALL, :])
            halves.append(jnp.dot(place_ref[...], jnp.concatenate(rows, axis=0), preferred_element_type=F32))
        return jnp.concatenate(halves, axis=1)

    cells = gather(0)
    center = jnp.mean(cells, axis=1, keepdims=True)
    cells = cells - center
    spread = jnp.mean(jnp.square(cells), axis=1, keepdims=True)
    inv_std = lax.rsqrt(spread + 1e-05)
    cells = cells * inv_std
    normed[...] = cells
    normed_bf[...] = cells.astype(BF)
    inv[...] = jnp.broadcast_to(inv_std, (288, 128))
    normed_t[...] = jnp.transpose(normed_bf[...], (1, 0))
    grads[...] = gather(1).astype(BF)
    grads_t[...] = jnp.transpose(grads[...], (1, 0))

    lane = lax.broadcasted_iota(jnp.int32, (WT, 128), 1)
    first = lane < HD

    def split(value):
        zero = jnp.zeros_like(value)
        return jnp.concatenate([jnp.where(first, value, zero), jnp.where(first, zero, value)], axis=0)

    for half in range(2):
        def weight(c):
            if half == 0:
                return wq_ref.at[c] if c < 3 else wp_ref
            return other_ref.at[c]

        for c in range(4):
            left = normed_bf if c < 3 else grads
            value = jnp.dot(left[...], weight(c)[...], preferred_element_type=F32)
            value = value.astype(BF)
            if c == 0:
                value = value * jnp.asarray(0.125, BF)
            parts[c] = value

        def pair(p, carry):
            span = pl.ds(pl.multiple_of(p * 128, 128), 128)
            for w in range(2):
                rows = pl.ds(w * WT, WT)
                q, k, v, g = (parts[c, rows, span] for c in range(4))
                qq, gg = split(q), split(g)
                bias = jnp.concatenate([bias_ref[half * 8 + 2 * p], bias_ref[half * 8 + 2 * p + 1]], axis=0)
                contract = (((1,), (1,)), ((), ()))
                flip = (((0,), (0,)), ((), ()))
                scores = lax.dot_general(qq, k, contract, preferred_element_type=F32) + bias
                weights = jnp.exp(scores)
                probs = weights / jnp.sum(weights, axis=1, keepdims=True)
                probs_bf = probs.astype(BF)
                found = jnp.dot(probs_bf, v, preferred_element_type=F32)
                att[rows, span] = jnp.where(first, found[0:WT], found[WT:]).astype(BF)
                gprobs = lax.dot_general(gg, v, contract, preferred_element_type=F32)
                dot_sum = jnp.sum(probs * gprobs, axis=1, keepdims=True)
                gscores = (probs * (gprobs - dot_sum)).astype(BF)
                gq = jnp.dot(gscores, k, preferred_element_type=F32)
                dparts[0, rows, span] = (jnp.where(first, gq[0:WT], gq[WT:]) * 0.125).astype(BF)
                dparts[1, rows, span] = lax.dot_general(gscores, qq, flip, preferred_element_type=F32).astype(BF)
                dparts[2, rows, span] = lax.dot_general(probs_bf, gg, flip, preferred_element_type=F32).astype(BF)
            return carry

        lax.fori_loop(0, 4, pair, 0)

        for c in range(3):
            value = lax.dot_general(dparts[c], weight(c)[...], (((1,), (1,)), ((), ())), preferred_element_type=F32)
            if half == 0 and c == 0:
                dx[...] = value
            else:
                dx[...] += value

        for c in range(4):
            left = normed_t if c < 3 else grads_t

            def block(r, carry):
                rows = pl.ds(pl.multiple_of(r * 256, 256), 256)
                right = dparts[c] if c < 3 else att[...]
                sums_ref[2 * c + half, rows, :] = jnp.dot(left[rows, :], right, preferred_element_type=F32).astype(BF)
                return carry

            lax.fori_loop(0, 4, block, 0)

    total = dx[...]
    mean_grad = jnp.mean(total, axis=1, keepdims=True)
    mean_cross = jnp.mean(total * normed[...], axis=1, keepdims=True)
    result = (inv[:, 0:1] * (total - mean_grad - normed[...] * mean_cross)).astype(BF)
    moved = jnp.dot(placet_ref[...], result, preferred_element_type=F32).astype(BF)
    for di in range(2):
        for t in range(2):
            back_ref[t, di] = moved[di * PIECE:(di + 1) * PIECE, t * 512:(t + 1) * 512]


def take_kernel(sums_ref, back_ref, packt_ref, tokens_ref, total_ref,
                landed, core_in, core_sum, xa_in, yb_in, xa_sum, yb_sum, ya_in, xb_in, z_out, z_in, t_out, t_in,
                piece_send, piece_recv, r_send, r_recv, local_sem):
    lat, lon, tp = position()
    x, zl, y, core, sibling, along_x, along_y, along_z, partner = neighbours()
    ends = piece_ends(1)
    sources = piece_ends(-1)
    enter([e[3] for e in sources] + [sibling, along_z, partner] + along_x + along_y)

    core_copy = send(sums_ref.at[:, :, 1 - core], core_in, r_send.at[0], r_recv.at[0], sibling)
    spans = (pl.ds(0, BIG), pl.ds(BIG, SMALL))
    pieces = []
    for n, (di, dj, to_tp, target) in enumerate(ends):
        pieces.append(send(back_ref.at[to_tp, di, spans[dj]], landed.at[tp, di, spans[dj]],
                           piece_send.at[n], piece_recv.at[n], target))
    own = pltpu.make_async_copy(back_ref.at[tp, 0, spans[0]], landed.at[tp, 0, spans[0]], local_sem)
    own.start()

    core_copy.wait()

    def add_core(n, carry):
        for k in range(4):
            rows = pl.ds(k * 8, 8)
            value = sums_ref[n, rows, core].astype(F32) + core_in[n, rows].astype(F32)
            core_sum[n, k] = value.reshape(2, 4, 16, 512).astype(BF)
        return carry

    lax.fori_loop(0, 8, add_core, 0)

    stage = []
    for d in range(3):
        stage.append(send(core_sum.at[0:4, (x + d + 1) % 4], xa_in.at[d], r_send.at[1 + d], r_recv.at[1 + d], along_x[d]))
        stage.append(send(core_sum.at[4:8, :, :, (y + d + 1) % 4], yb_in.at[d], r_send.at[4 + d], r_recv.at[4 + d], along_y[d]))
    for copy in stage:
        copy.wait()

    def add_first(n, carry):
        value = core_sum[n, x].astype(F32)
        for d in range(3):
            value += xa_in[d, n].astype(F32)
        xa_sum[n] = value.astype(BF)
        value = core_sum[4 + n, :, :, y].astype(F32)
        for d in range(3):
            value += yb_in[d, n].astype(F32)
        yb_sum[n] = value.astype(BF)
        return carry

    lax.fori_loop(0, 4, add_first, 0)

    stage = []
    for d in range(3):
        stage.append(send(xa_sum.at[:, :, (y + d + 1) % 4], ya_in.at[d], r_send.at[7 + d], r_recv.at[7 + d], along_y[d]))
        stage.append(send(yb_sum.at[:, (x + d + 1) % 4], xb_in.at[d], r_send.at[10 + d], r_recv.at[10 + d], along_x[d]))
    for copy in stage:
        copy.wait()

    def add_second(n, carry):
        value = xa_sum[n, :, y].astype(F32)
        for d in range(3):
            value += ya_in[d, n].astype(F32)
        z_out[n] = value.astype(BF)
        value = yb_sum[n, x].astype(F32)
        for d in range(3):
            value += xb_in[d, n].astype(F32)
        z_out[4 + n] = value.astype(BF)
        return carry

    lax.fori_loop(0, 4, add_second, 0)

    z_copy = send(z_out.at[:, 1 - zl], z_in, r_send.at[13], r_recv.at[13], along_z)
    z_copy.wait()
    for c in range(4):
        t_out[c] = (z_out[2 * c + 1, zl].astype(F32) + z_in[2 * c + 1].astype(F32)).astype(BF)
    t_copy = send(t_out, t_in, r_send.at[14], r_recv.at[14], partner)

    own.wait()
    for copy in pieces:
        copy.wait()
    for t in range(2):
        cells = landed[t].reshape(2 * PIECE, 512)
        moved = jnp.dot(packt_ref[...], cells, preferred_element_type=F32).astype(BF)
        if t == 0:
            tokens_ref[144:432, :] = moved
        else:
            tokens_ref[432:576, :] = moved[0:144]
            tokens_ref[0:144, :] = moved[144:288]

    t_copy.wait()
    for c in range(4):
        total_ref[c] = z_out[2 * c, zl].astype(F32) + z_in[2 * c].astype(F32) + t_in[c].astype(F32)


VM = pl.BlockSpec(memory_space=pltpu.VMEM)
SM = pl.BlockSpec(memory_space=pltpu.SMEM)
LIMIT = 56 * 1024 * 1024


def shards(tokens, w_qkv, w_proj, bias_table, bias_index, regions, out_grad):
    flat_in = tokens.reshape(576, 512)
    flat_grad = out_grad.reshape(576, 512)
    wq = w_qkv.transpose(1, 0, 2)
    pack = jnp.asarray(PACK, BF)
    packt = jnp.asarray(np.concatenate([PACK[0].T, PACK[1].T], axis=1), BF)
    place = jnp.asarray(PLACE, BF)
    placet = jnp.asarray(PLACE.T, BF)
    dma = pltpu.SemaphoreType.DMA
    shape = jax.ShapeDtypeStruct
    held, other, tables = pl.pallas_call(
        bring_kernel,
        out_shape=(
            shape((2, 2, 2 * PIECE, 512), BF),
            shape((4, 4, 2, 4, 2, 16, 512), BF),
            shape((2, 8, 768), F32),
        ),
        in_specs=[VM] * 6,
        out_specs=(VM, VM, VM),
        scratch_shapes=[
            pltpu.VMEM((2, 2, 2 * PIECE, 512), BF),
            dma((7,)), dma((7,)), dma((17,)), dma((17,)), dma,
        ],
        compiler_params=pltpu.CompilerParams(collective_id=0, has_side_effects=True, vmem_limit_bytes=LIMIT),
        name="bring",
    )(flat_in, flat_grad, pack, wq.reshape(3, 64, 16, 512), w_proj.reshape(64, 16, 512), bias_table.T)

    bias = pl.pallas_call(
        bias_kernel,
        out_shape=shape((16, WT, WT), F32),
        in_specs=[VM, VM, SM],
        out_specs=VM,
        compiler_params=pltpu.CompilerParams(vmem_limit_bytes=LIMIT),
        name="bias",
    )(tables, bias_index, regions)

    vmem = pltpu.VMEM
    sums, back = pl.pallas_call(
        work_kernel,
        out_shape=(shape((8, 1024, 512), BF), shape((2, 2, PIECE, 512), BF)),
        in_specs=[VM] * 7,
        out_specs=(VM, VM),
        scratch_shapes=[
            vmem((288, 1024), F32), vmem((288, 1024), BF), vmem((288, 1024), BF), vmem((1024, 288), BF),
            vmem((1024, 288), BF), vmem((288, 128), F32), vmem((4, 288, 512), BF), vmem((3, 288, 512), BF),
            vmem((288, 512), BF), vmem((288, 1024), F32),
        ],
        compiler_params=pltpu.CompilerParams(vmem_limit_bytes=LIMIT),
        name="work",
    )(held, place, placet, wq, w_proj, other.reshape(4, 1024, 512), bias)

    grad_tokens, total = pl.pallas_call(
        take_kernel,
        out_shape=(shape((576, 512), BF), shape((4, 16, 512), F32)),
        in_specs=[VM] * 3,
        out_specs=(VM, VM),
        scratch_shapes=[
            vmem((2, 2, PIECE, 512), BF),
            vmem((8, 32, 16, 512), BF), vmem((8, 4, 2, 4, 16, 512), BF),
            vmem((3, 4, 2, 4, 16, 512), BF), vmem((3, 4, 4, 2, 16, 512), BF),
            vmem((4, 2, 4, 16, 512), BF), vmem((4, 4, 2, 16, 512), BF),
            vmem((3, 4, 2, 16, 512), BF), vmem((3, 4, 2, 16, 512), BF),
            vmem((8, 2, 16, 512), BF), vmem((8, 16, 512), BF),
            vmem((4, 16, 512), BF), vmem((4, 16, 512), BF),
            dma((7,)), dma((7,)), dma((15,)), dma((15,)), dma,
        ],
        compiler_params=pltpu.CompilerParams(collective_id=1, has_side_effects=True, vmem_limit_bytes=LIMIT),
        name="take",
    )(sums.reshape(8, 32, 2, 16, 512), back, packt)

    qkv_grad = total[0:3].transpose(1, 0, 2)
    proj_grad = total[3]
    return grad_tokens.reshape(tokens.shape), qkv_grad, proj_grad


def solution(mesh):
    in_specs = (
        P(None, "lat", "lon", "tp"),
        P(None, None, "tp"),
        P(None, "tp"),
        P(None, "tp"),
        P(),
        P(None, "lat", "lon"),
        P(None, "lat", "lon", "tp"),
    )
    out_specs = (
        P(None, "lat", "lon", "tp"),
        P(("lat", "lon"), None, "tp"),
        P(("lat", "lon"), "tp"),
    )
    return jax.shard_map(shards, mesh=mesh, in_specs=in_specs, out_specs=out_specs, check_vma=False)
```

```python
import functools

import jax
import jax.numpy as jnp
import numpy as np
from jax import lax
from jax.experimental import pallas as pl
from jax.experimental.pallas import tpu as pltpu
from jax.sharding import PartitionSpec as P

HD = 64
WT = 144
BIG = 112
SMALL = 48
PIECE = BIG + SMALL
MESH = pl.DeviceIdType.MESH
BF = jnp.bfloat16
F32 = jnp.float32
FAR = -1e30


def permutations():
    pack = np.zeros((2, PIECE, 288), np.float32)
    place = np.zeros((288, 2 * PIECE), np.float32)
    for di in range(2):
        for lv in range(2):
            for row in range(3):
                local = row + (3 if di == 0 else 0)
                for col in range(24):
                    if col >= 6:
                        spot = lv * 54 + row * 18 + col - 6
                    else:
                        spot = BIG + lv * 18 + row * 6 + col
                    pack[di, spot, lv * 144 + local * 24 + col] = 1
                    shifted = (col - 6) % 24
                    cell = (shifted // 12) * 144 + lv * 72 + (row + 3 * di) * 12 + shifted % 12
                    place[cell, di * PIECE + spot] = 1
    return pack, place


PACK, PLACE = permutations()


def position():
    lat, lon, tp = lax.axis_index("lat"), lax.axis_index("lon"), lax.axis_index("tp")
    return lat, lon, tp


def device(lat, lon, tp):
    return {"lat": lat, "lon": lon, "tp": tp}


def neighbours():
    lat, lon, tp = position()
    x, zl, y, core = lat // 2, lat % 2, lon // 2, lon % 2
    sibling = device(lat, y * 2 + 1 - core, tp)
    along_x = [device(((x + d) % 4) * 2 + zl, lon, tp) for d in (1, 2, 3)]
    along_y = [device(lat, ((y + d) % 4) * 2 + core, tp) for d in (1, 2, 3)]
    along_z = device(x * 2 + 1 - zl, lon, tp)
    partner = device(lat, lon, 1 - tp)
    return x, zl, y, core, sibling, along_x, along_y, along_z, partner


def piece_ends(sign):
    lat, lon, tp = position()
    ends = []
    for di in range(2):
        for dj in range(2):
            for other in range(2):
                if di == 0 and dj == 0 and other == 0:
                    continue
                to_tp = 1 - tp if other else tp
                ends.append((di, dj, to_tp, device((lat + sign * di + 8) % 8, (lon + sign * dj + 8) % 8, to_tp)))
    return ends


def send(src, dst, send_sem, recv_sem, target):
    copy = pltpu.make_async_remote_copy(
        src_ref=src, dst_ref=dst, send_sem=send_sem, recv_sem=recv_sem, device_id=target, device_id_type=MESH
    )
    copy.start()
    return copy


def whole_kernel(tok_ref, grad_ref, pack_ref, place_ref, placet_ref, wq_hbm, wp_hbm, table_ref, index_ref, regions_ref,
                 landed, total_ref,
                 wq_ref, wp_ref, other_ref, tables_ref, packed, held, bias_ref,
                 normed, normed_bf, grads, normed_t, grads_t, inv, parts, dparts, att, dx, back,
                 sums, core_in, core_sum, xa_in, yb_in, xa_sum, yb_sum, ya_in, xb_in, z_out, z_in, t_out, t_in,
                 piece_send, piece_recv, back_send, back_recv, w_send, w_recv, r_send, r_recv, local_sem):
    lat, lon, tp = position()
    x, zl, y, core, sibling, along_x, along_y, along_z, partner = neighbours()
    ahead, behind = piece_ends(-1), piece_ends(1)
    barrier = pltpu.get_barrier_semaphore()
    targets = [e[3] for e in ahead] + [e[3] for e in behind] + [sibling, along_z, partner] + along_x + along_y
    for target in targets:
        pl.semaphore_signal(barrier, inc=1, device_id=target, device_id_type=MESH)

    own_weights = [
        pltpu.make_async_copy(wq_hbm, wq_ref, local_sem.at[0]),
        pltpu.make_async_copy(wp_hbm, wp_ref, local_sem.at[1]),
    ]
    for copy in own_weights:
        copy.start()

    tables_ref[0] = jnp.zeros((8, 768), F32)
    tables_ref[0, :, 0:759] = table_ref[...]

    def pack(half):
        for di in range(2):
            for which, ref in enumerate((tok_ref, grad_ref)):
                if half == 0:
                    cells = ref[144:432, :]
                else:
                    cells = jnp.concatenate([ref[432:576, :], ref[0:144, :]], axis=0)
                moved = jnp.dot(pack_ref[di], cells, preferred_element_type=F32).astype(BF)
                packed[half, di, which * BIG:(which + 1) * BIG, :] = moved[0:BIG]
                base = 2 * BIG + which * SMALL
                packed[half, di, base:base + SMALL, :] = moved[BIG:PIECE]

    pack(0)
    pack(1)
    pl.semaphore_wait(barrier, len(targets))

    mine = ((x * 2 + zl) * 4 + y) * 2 + core
    first = [
        send(wq_hbm.at[:, mine], other_ref.at[0:3, x, zl, y, core], w_send.at[0], w_recv.at[0], partner),
        send(wp_hbm.at[mine], other_ref.at[3, x, zl, y, core], w_send.at[1], w_recv.at[1], partner),
        send(tables_ref.at[0], tables_ref.at[1], w_send.at[2], w_recv.at[2], partner),
    ]
    spans = (pl.ds(0, 2 * BIG), pl.ds(2 * BIG, 2 * SMALL))
    pieces = []
    for n, (di, dj, to_tp, target) in enumerate(ahead):
        pieces.append(send(packed.at[to_tp, di, spans[dj]], held.at[tp, di, spans[dj]],
                           piece_send.at[n], piece_recv.at[n], target))
    own = pltpu.make_async_copy(packed.at[tp, 0, spans[0]], held.at[tp, 0, spans[0]], local_sem.at[2])
    own.start()
    pieces.append(own)

    rows = lax.broadcasted_iota(jnp.int32, (WT, WT), 0) // 12
    cols = lax.broadcasted_iota(jnp.int32, (WT, WT), 1) // 12
    left = jnp.zeros((WT, WT), jnp.int32)
    right = jnp.zeros((WT, WT), jnp.int32)
    for lv in range(2):
        for row in range(6):
            value = regions_ref[row, pl.ds(2 * tp + lv, 1), 0:1]
            left = jnp.where(rows == lv * 6 + row, value, left)
            right = jnp.where(cols == lv * 6 + row, value, right)
    blocked = jnp.where(left == right, 0.0, FAR).astype(F32)

    for copy in first:
        copy.wait()
    second = send(other_ref.at[:, x, zl, y, core], other_ref.at[:, x, zl, y, core], w_send.at[3], w_recv.at[3], along_z)

    blocks = []
    for s in range(2):
        table = tables_ref[s]
        top = table.astype(BF).astype(F32)
        rest = table - top
        mid = rest.astype(BF).astype(F32)
        low = rest - mid
        for part in (top, mid, low):
            for g in range(3):
                blocks.append(part[:, g * 256:(g + 1) * 256])
    matrix = jnp.concatenate(blocks, axis=0).astype(BF)
    depth = lax.broadcasted_iota(jnp.int32, (256, WT), 0)

    def some_rows(step, carry):
        found = ([], [])
        index = index_ref[pl.ds(pl.multiple_of(step * 8, 8), 8), :]
        for r in range(8):
            row = index[r:r + 1, :]
            low_part, high_part = row & 255, row >> 8
            hot = jnp.where(depth == low_part, 1.0, 0.0).astype(BF)
            picked = jnp.dot(matrix, hot, preferred_element_type=F32)
            for s in range(2):
                total = jnp.zeros((8, WT), F32)
                for g in range(3):
                    base = s * 72 + g * 8
                    value = picked[base:base + 8] + picked[base + 24:base + 32] + picked[base + 48:base + 56]
                    total = jnp.where(high_part == g, value, total)
                found[s].append(total)
        for s in range(2):
            stacked = jnp.stack(found[s], axis=0)
            bias_ref[s * 8:(s + 1) * 8, pl.ds(pl.multiple_of(step * 8, 8), 8), :] = jnp.transpose(stacked, (1, 0, 2))
        return carry

    lax.fori_loop(0, 9, some_rows, 0)
    second.wait()
    third = []
    for d in range(3):
        third.append(send(other_ref.at[0:2, x, :, y, core], other_ref.at[0:2, x, :, y, core],
                          w_send.at[4 + d], w_recv.at[4 + d], along_x[d]))
        third.append(send(other_ref.at[2:4, x, :, y, core], other_ref.at[2:4, x, :, y, core],
                          w_send.at[7 + d], w_recv.at[7 + d], along_y[d]))
    lax.fori_loop(9, WT // 8, some_rows, 0)
    for h in range(16):
        bias_ref[h] = bias_ref[h] + blocked

    for copy in pieces:
        copy.wait()

    def gather(which):
        halves = []
        for t in range(2):
            rows = []
            for di in range(2):
                rows.append(held[t, di, which * BIG:(which + 1) * BIG, :])
                base = 2 * BIG + which * SMALL
                rows.append(held[t, di, base:base + SMALL, :])
            halves.append(jnp.dot(place_ref[...], jnp.concatenate(rows, axis=0), preferred_element_type=F32))
        return jnp.concatenate(halves, axis=1)

    cells = gather(0)
    center = jnp.mean(cells, axis=1, keepdims=True)
    cells = cells - center
    spread = jnp.mean(jnp.square(cells), axis=1, keepdims=True)
    inv_std = lax.rsqrt(spread + 1e-05)
    cells = cells * inv_std
    normed[...] = cells
    normed_bf[...] = cells.astype(BF)
    inv[...] = jnp.broadcast_to(inv_std, (288, 128))
    normed_t[...] = jnp.transpose(normed_bf[...], (1, 0))
    grads[...] = gather(1).astype(BF)
    grads_t[...] = jnp.transpose(grads[...], (1, 0))

    for copy in third:
        copy.wait()
    fourth = []
    for d in range(3):
        fourth.append(send(other_ref.at[0:2, :, :, y, core], other_ref.at[0:2, :, :, y, core],
                           w_send.at[10 + d], w_recv.at[10 + d], along_y[d]))
        fourth.append(send(other_ref.at[2:4, x, :, :, core], other_ref.at[2:4, x, :, :, core],
                           w_send.at[13 + d], w_recv.at[13 + d], along_x[d]))
    for copy in own_weights:
        copy.wait()

    lane = lax.broadcasted_iota(jnp.int32, (WT, 128), 1)
    lower = lane < HD

    def split(value):
        zero = jnp.zeros_like(value)
        return jnp.concatenate([jnp.where(lower, value, zero), jnp.where(lower, zero, value)], axis=0)

    def weight(half, c):
        if half == 0:
            return (wq_ref[c] if c < 3 else wp_ref[...]).reshape(1024, 512)
        return other_ref[c].reshape(1024, 512)

    def project(half):
        for c in range(4):
            left = normed_bf if c < 3 else grads
            value = jnp.dot(left[...], weight(half, c), preferred_element_type=F32)
            value = value.astype(BF)
            if c == 0:
                value = value * jnp.asarray(0.125, BF)
            parts[c] = value

    def attend(half):
        def pair(p, carry):
            span = pl.ds(pl.multiple_of(p * 128, 128), 128)
            for w in range(2):
                rows = pl.ds(w * WT, WT)
                q, k, v, g = (parts[c, rows, span] for c in range(4))
                qq, gg = split(q), split(g)
                bias = jnp.concatenate([bias_ref[half * 8 + 2 * p], bias_ref[half * 8 + 2 * p + 1]], axis=0)
                contract = (((1,), (1,)), ((), ()))
                flip = (((0,), (0,)), ((), ()))
                scores = lax.dot_general(qq, k, contract, preferred_element_type=F32) + bias
                weights = jnp.exp(scores)
                probs = weights / jnp.sum(weights, axis=1, keepdims=True)
                probs_bf = probs.astype(BF)
                found = jnp.dot(probs_bf, v, preferred_element_type=F32)
                att[rows, span] = jnp.where(lower, found[0:WT], found[WT:]).astype(BF)
                gprobs = lax.dot_general(gg, v, contract, preferred_element_type=F32)
                dot_sum = jnp.sum(probs * gprobs, axis=1, keepdims=True)
                gscores = (probs * (gprobs - dot_sum)).astype(BF)
                gq = jnp.dot(gscores, k, preferred_element_type=F32)
                dparts[0, rows, span] = (jnp.where(lower, gq[0:WT], gq[WT:]) * 0.125).astype(BF)
                dparts[1, rows, span] = lax.dot_general(gscores, qq, flip, preferred_element_type=F32).astype(BF)
                dparts[2, rows, span] = lax.dot_general(probs_bf, gg, flip, preferred_element_type=F32).astype(BF)
            return carry

        lax.fori_loop(0, 4, pair, 0)

    def input_grad(half):
        for c in range(3):
            value = lax.dot_general(dparts[c], weight(half, c), (((1,), (1,)), ((), ())), preferred_element_type=F32)
            if half == 0 and c == 0:
                dx[...] = value
            else:
                dx[...] += value

    def weight_grad(half):
        copies = []
        for c in range(4):
            left = normed_t if c < 3 else grads_t

            def block(r, carry):
                rows = pl.ds(pl.multiple_of(r * 256, 256), 256)
                right = dparts[c] if c < 3 else att[...]
                value = jnp.dot(left[rows, :], right, preferred_element_type=F32).astype(BF)
                sums[half, c, pl.ds(r * 8, 8)] = value.reshape(8, 2, 16, 512)
                return carry

            lax.fori_loop(0, 4, block, 0)
            copies.append(send(sums.at[half, c, :, 1 - core], core_in.at[half, c],
                               r_send.at[half, c], r_recv.at[half, c], sibling))
        return copies

    def reduce_first(half, copies):
        for copy in copies:
            copy.wait()

        def add(n, carry):
            for k in range(4):
                rows = pl.ds(k * 8, 8)
                value = sums[half, n, rows, core].astype(F32) + core_in[half, n, rows].astype(F32)
                core_sum[half, n, k] = value.reshape(2, 4, 16, 512).astype(BF)
            return carry

        lax.fori_loop(0, 4, add, 0)
        stage = []
        for d in range(3):
            stage.append(send(core_sum.at[half, 0:2, (x + d + 1) % 4], xa_in.at[half, d],
                              r_send.at[half, 4 + d], r_recv.at[half, 4 + d], along_x[d]))
            stage.append(send(core_sum.at[half, 2:4, :, :, (y + d + 1) % 4], yb_in.at[half, d],
                              r_send.at[half, 7 + d], r_recv.at[half, 7 + d], along_y[d]))
        return stage

    def reduce_second(half, copies):
        for copy in copies:
            copy.wait()
        for n in range(2):
            value = core_sum[half, n, x].astype(F32)
            for d in range(3):
                value += xa_in[half, d, n].astype(F32)
            xa_sum[half, n] = value.astype(BF)
            value = core_sum[half, 2 + n, :, :, y].astype(F32)
            for d in range(3):
                value += yb_in[half, d, n].astype(F32)
            yb_sum[half, n] = value.astype(BF)
        stage = []
        for d in range(3):
            stage.append(send(xa_sum.at[half, :, :, (y + d + 1) % 4], ya_in.at[half, d],
                              r_send.at[half, 10 + d], r_recv.at[half, 10 + d], along_y[d]))
            stage.append(send(yb_sum.at[half, :, (x + d + 1) % 4], xb_in.at[half, d],
                              r_send.at[half, 13 + d], r_recv.at[half, 13 + d], along_x[d]))
        return stage

    def reduce_third(half, copies):
        for copy in copies:
            copy.wait()
        for n in range(2):
            value = xa_sum[half, n, :, y].astype(F32)
            for d in range(3):
                value += ya_in[half, d, n].astype(F32)
            z_out[half, n] = value.astype(BF)
            value = yb_sum[half, n, x].astype(F32)
            for d in range(3):
                value += xb_in[half, d, n].astype(F32)
            z_out[half, 2 + n] = value.astype(BF)
        return [send(z_out.at[half, :, 1 - zl], z_in.at[half], r_send.at[half, 16], r_recv.at[half, 16], along_z)]

    project(0)
    attend(0)
    for copy in fourth:
        copy.wait()
    fifth = send(other_ref.at[:, :, :, :, core], other_ref.at[:, :, :, :, core], w_send.at[16], w_recv.at[16], sibling)
    near = weight_grad(0)
    input_grad(0)
    fifth.wait()
    project(1)
    near = reduce_first(0, near)
    attend(1)
    near = reduce_second(0, near)
    far = weight_grad(1)
    input_grad(1)

    total = dx[...]
    mean_grad = jnp.mean(total, axis=1, keepdims=True)
    mean_cross = jnp.mean(total * normed[...], axis=1, keepdims=True)
    result = (inv[:, 0:1] * (total - mean_grad - normed[...] * mean_cross)).astype(BF)
    moved = jnp.dot(placet_ref[...], result, preferred_element_type=F32).astype(BF)
    for di in range(2):
        for t in range(2):
            back[t, di] = moved[di * PIECE:(di + 1) * PIECE, t * 512:(t + 1) * 512]

    far = reduce_first(1, far)
    spans = (pl.ds(0, BIG), pl.ds(BIG, SMALL))
    pieces = []
    for n, (di, dj, to_tp, target) in enumerate(behind):
        pieces.append(send(back.at[to_tp, di, spans[dj]], landed.at[tp, di, spans[dj]],
                           back_send.at[n], back_recv.at[n], target))
    own = pltpu.make_async_copy(back.at[tp, 0, spans[0]], landed.at[tp, 0, spans[0]], local_sem.at[3])
    own.start()
    pieces.append(own)
    near = reduce_third(0, near)
    far = reduce_second(1, far)
    far = reduce_third(1, far)
    for copy in near + far:
        copy.wait()
    for c in range(4):
        t_out[c] = (z_out[1, c, zl].astype(F32) + z_in[1, c].astype(F32)).astype(BF)
    last = send(t_out, t_in, r_send.at[0, 17], r_recv.at[0, 17], partner)
    for copy in pieces:
        copy.wait()
    last.wait()
    for c in range(4):
        total_ref[c] = z_out[0, c, zl].astype(F32) + z_in[0, c].astype(F32) + t_in[c].astype(F32)


def finish_kernel(landed, total_ref, packt_ref, tokens_ref, qkv_ref, proj_ref):
    for t in range(2):
        cells = landed[t].reshape(2 * PIECE, 512)
        moved = jnp.dot(packt_ref[...], cells, preferred_element_type=F32).astype(BF)
        if t == 0:
            tokens_ref[144:432, :] = moved
        else:
            tokens_ref[432:576, :] = moved[0:144]
            tokens_ref[0:144, :] = moved[144:288]
    qkv_ref[...] = total_ref[0:3]
    proj_ref[...] = total_ref[3]


VM = pl.BlockSpec(memory_space=pltpu.VMEM)
HB = pl.BlockSpec(memory_space=pl.ANY)
LIMIT = 60 * 1024 * 1024


def shards(tokens, w_qkv, w_proj, bias_table, bias_index, regions, out_grad):
    flat_in = tokens.reshape(576, 512)
    flat_grad = out_grad.reshape(576, 512)
    wq = w_qkv.transpose(1, 0, 2).reshape(3, 64, 16, 512)
    wp = w_proj.reshape(64, 16, 512)
    pack = jnp.asarray(PACK, BF)
    packt = jnp.asarray(np.concatenate([PACK[0].T, PACK[1].T], axis=1), BF)
    place = jnp.asarray(PLACE, BF)
    placet = jnp.asarray(PLACE.T, BF)
    dma = pltpu.SemaphoreType.DMA
    shape = jax.ShapeDtypeStruct
    vmem = pltpu.VMEM
    landed, total = pl.pallas_call(
        whole_kernel,
        out_shape=(shape((2, 2, PIECE, 512), BF), shape((4, 16, 512), F32)),
        in_specs=[VM] * 5 + [HB] * 2 + [VM] * 3,
        out_specs=(VM, VM),
        scratch_shapes=[
            vmem((3, 64, 16, 512), BF), vmem((64, 16, 512), BF),
            vmem((4, 4, 2, 4, 2, 16, 512), BF), vmem((2, 8, 768), F32),
            vmem((2, 2, 2 * PIECE, 512), BF), vmem((2, 2, 2 * PIECE, 512), BF), vmem((16, WT, WT), F32),
            vmem((288, 1024), F32), vmem((288, 1024), BF), vmem((288, 1024), BF), vmem((1024, 288), BF),
            vmem((1024, 288), BF), vmem((288, 128), F32), vmem((4, 288, 512), BF), vmem((3, 288, 512), BF),
            vmem((288, 512), BF), vmem((288, 1024), F32), vmem((2, 2, PIECE, 512), BF),
            vmem((2, 4, 32, 2, 16, 512), BF), vmem((2, 4, 32, 16, 512), BF), vmem((2, 4, 4, 2, 4, 16, 512), BF),
            vmem((2, 3, 2, 2, 4, 16, 512), BF), vmem((2, 3, 2, 4, 2, 16, 512), BF),
            vmem((2, 2, 2, 4, 16, 512), BF), vmem((2, 2, 4, 2, 16, 512), BF),
            vmem((2, 3, 2, 2, 16, 512), BF), vmem((2, 3, 2, 2, 16, 512), BF),
            vmem((2, 4, 2, 16, 512), BF), vmem((2, 4, 16, 512), BF),
            vmem((4, 16, 512), BF), vmem((4, 16, 512), BF),
            dma((7,)), dma((7,)), dma((7,)), dma((7,)), dma((17,)), dma((17,)), dma((2, 18)), dma((2, 18)), dma((4,)),
        ],
        compiler_params=pltpu.CompilerParams(collective_id=0, has_side_effects=True, vmem_limit_bytes=LIMIT),
        name="whole",
    )(flat_in, flat_grad, pack, place, placet, wq, wp, bias_table.T, bias_index, regions.transpose(1, 0, 2))

    grad_tokens, qkv_grad, proj_grad = pl.pallas_call(
        finish_kernel,
        out_shape=(shape((576, 512), BF), shape((3, 16, 512), F32), shape((16, 512), F32)),
        in_specs=[VM] * 3,
        out_specs=(VM, VM, VM),
        name="finish",
    )(landed, total, packt)
    return grad_tokens.reshape(tokens.shape), qkv_grad.transpose(1, 0, 2), proj_grad


def solution(mesh):
    in_specs = (
        P(None, "lat", "lon", "tp"),
        P(None, None, "tp"),
        P(None, "tp"),
        P(None, "tp"),
        P(),
        P(None, "lat", "lon"),
        P(None, "lat", "lon", "tp"),
    )
    out_specs = (
        P(None, "lat", "lon", "tp"),
        P(("lat", "lon"), None, "tp"),
        P(("lat", "lon"), "tp"),
    )
    return jax.shard_map(shards, mesh=mesh, in_specs=in_specs, out_specs=out_specs, check_vma=False)
```

```python
import functools

import jax
import jax.numpy as jnp
import numpy as np
from jax import lax
from jax.experimental import pallas as pl
from jax.experimental.pallas import tpu as pltpu
from jax.sharding import PartitionSpec as P

HD = 64
WT = 144
BIG = 112
SMALL = 48
PIECE = BIG + SMALL
BOTH_BIG = 224
BOTH_SMALL = 80
BOTH = BOTH_BIG + BOTH_SMALL
MESH = pl.DeviceIdType.MESH
BF = jnp.bfloat16
F32 = jnp.float32
FAR = -1e30


def permutations():
    pack = np.zeros((2, BOTH, 576), np.float32)
    place = np.zeros((2, 288, 2 * BOTH), np.float32)
    leave = np.zeros((2 * PIECE, 288), np.float32)
    unpack = np.zeros((288, 2 * PIECE), np.float32)
    for di in range(2):
        for lv in range(2):
            for row in range(3):
                local = row + (3 if di == 0 else 0)
                for col in range(24):
                    cell = lv * 144 + local * 24 + col
                    shifted = (col - 6) % 24
                    window = (shifted // 12) * 144 + lv * 72 + (row + 3 * di) * 12 + shifted % 12
                    big = lv * 54 + row * 18 + col - 6
                    small = lv * 18 + row * 6 + col
                    for which in range(2):
                        spot = which * 108 + big if col >= 6 else BOTH_BIG + which * 36 + small
                        pack[di, spot, which * 288 + cell] = 1
                        place[which, window, di * BOTH + spot] = 1
                    spot = big if col >= 6 else BIG + small
                    leave[di * PIECE + spot, window] = 1
                    unpack[cell, di * PIECE + spot] = 1
    return pack, place, leave, unpack


PACK, PLACE, LEAVE, UNPACK = permutations()


def position():
    lat, lon, tp = lax.axis_index("lat"), lax.axis_index("lon"), lax.axis_index("tp")
    return lat, lon, tp


def device(lat, lon, tp):
    return {"lat": lat, "lon": lon, "tp": tp}


def neighbours():
    lat, lon, tp = position()
    x, zl, y, core = lat // 2, lat % 2, lon // 2, lon % 2
    sibling = device(lat, y * 2 + 1 - core, tp)
    along_x = [device(((x + d) % 4) * 2 + zl, lon, tp) for d in (1, 2, 3)]
    along_y = [device(lat, ((y + d) % 4) * 2 + core, tp) for d in (1, 2, 3)]
    along_z = device(x * 2 + 1 - zl, lon, tp)
    partner = device(lat, lon, 1 - tp)
    return x, zl, y, core, sibling, along_x, along_y, along_z, partner


def piece_ends(sign):
    lat, lon, tp = position()
    ends = []
    for di in range(2):
        for dj in range(2):
            for other in range(2):
                if di == 0 and dj == 0 and other == 0:
                    continue
                to_tp = 1 - tp if other else tp
                ends.append((di, dj, to_tp, device((lat + sign * di + 8) % 8, (lon + sign * dj + 8) % 8, to_tp)))
    return ends


def send(src, dst, send_sem, recv_sem, target):
    copy = pltpu.make_async_remote_copy(
        src_ref=src, dst_ref=dst, send_sem=send_sem, recv_sem=recv_sem, device_id=target, device_id_type=MESH
    )
    copy.start()
    return copy


def whole_kernel(tok_ref, grad_ref, pack_ref, place_ref, placet_ref, wq_hbm, wp_hbm, table_ref, index_ref, regions_ref,
                 landed, total_ref,
                 wq_ref, wp_ref, other_ref, tables_ref, packed, held, bias_ref,
                 normed, normed_bf, grads, normed_t, grads_t, both_x, both_g, inv, parts, dparts, dx, back,
                 *rest):
    groups, (t_out, t_in), sems = (rest[0:9], rest[9:18], rest[18:27]), rest[27:29], rest[29:]
    (piece_send, piece_recv, back_send, back_recv, w_send, w_recv, r_send, r_recv, t_send, t_recv, local_sem) = sems
    lat, lon, tp = position()
    x, zl, y, core, sibling, along_x, along_y, along_z, partner = neighbours()
    ahead, behind = piece_ends(-1), piece_ends(1)
    barrier = pltpu.get_barrier_semaphore()
    targets = [e[3] for e in ahead] + [e[3] for e in behind] + [sibling, along_z, partner] + along_x + along_y
    for target in targets:
        pl.semaphore_signal(barrier, inc=1, device_id=target, device_id_type=MESH)

    own_weights = [
        pltpu.make_async_copy(wq_hbm, wq_ref, local_sem.at[0]),
        pltpu.make_async_copy(wp_hbm, wp_ref, local_sem.at[1]),
    ]
    for copy in own_weights:
        copy.start()

    tables_ref[0] = jnp.zeros((8, 768), F32)
    tables_ref[0, :, 0:759] = table_ref[...]

    def pack(half):
        cells = []
        for ref in (tok_ref, grad_ref):
            if half == 0:
                cells.append(ref[144:432, :])
            else:
                cells.extend([ref[432:576, :], ref[0:144, :]])
        cells = jnp.concatenate(cells, axis=0)
        for di in range(2):
            packed[half, di] = jnp.dot(pack_ref[di], cells, preferred_element_type=F32).astype(BF)

    pack(0)
    pack(1)
    pl.semaphore_wait(barrier, len(targets))

    mine = (x * 4 + y) * 2 + core
    first = [
        send(wq_hbm.at[:, mine], other_ref.at[0:3, x, y, core], w_send.at[0], w_recv.at[0], partner),
        send(wp_hbm.at[mine], other_ref.at[3, x, y, core], w_send.at[1], w_recv.at[1], partner),
        send(tables_ref.at[0], tables_ref.at[1], w_send.at[2], w_recv.at[2], partner),
    ]
    spans = (pl.ds(0, BOTH_BIG), pl.ds(BOTH_BIG, BOTH_SMALL))
    pieces = []
    for n, (di, dj, to_tp, target) in enumerate(ahead):
        pieces.append(send(packed.at[to_tp, di, spans[dj]], held.at[tp, di, spans[dj]],
                           piece_send.at[n], piece_recv.at[n], target))
    own = pltpu.make_async_copy(packed.at[tp, 0, spans[0]], held.at[tp, 0, spans[0]], local_sem.at[2])
    own.start()
    pieces.append(own)

    for half in range(2):
        for c in range(4):
            for base in (288, 672):
                dparts[half, c, base:base + 96] = jnp.zeros((96, 512), BF)

    rows = lax.broadcasted_iota(jnp.int32, (WT, WT), 0) // 12
    cols = lax.broadcasted_iota(jnp.int32, (WT, WT), 1) // 12
    left = jnp.zeros((WT, WT), jnp.int32)
    right = jnp.zeros((WT, WT), jnp.int32)
    for lv in range(2):
        for row in range(6):
            value = regions_ref[row, pl.ds(2 * tp + lv, 1), 0:1]
            left = jnp.where(rows == lv * 6 + row, value, left)
            right = jnp.where(cols == lv * 6 + row, value, right)
    blocked = jnp.where(left == right, 0.0, FAR).astype(F32)

    first.pop().wait()
    blocks = []
    for s in range(2):
        table = tables_ref[s]
        top = table.astype(BF).astype(F32)
        rest = table - top
        mid = rest.astype(BF).astype(F32)
        low = rest - mid
        for part in (top, mid, low):
            for g in range(3):
                blocks.append(part[:, g * 256:(g + 1) * 256])
    matrix = jnp.concatenate(blocks, axis=0).astype(BF)
    depth = lax.broadcasted_iota(jnp.int32, (256, WT), 0)

    def some_rows(step, carry):
        found = ([], [])
        index = index_ref[pl.ds(pl.multiple_of(step * 8, 8), 8), :]
        for r in range(8):
            row = index[r:r + 1, :]
            low_part, high_part = row & 255, row >> 8
            hot = jnp.where(depth == low_part, 1.0, 0.0).astype(BF)
            picked = jnp.dot(matrix, hot, preferred_element_type=F32)
            for s in range(2):
                total = jnp.zeros((8, WT), F32)
                for g in range(3):
                    base = s * 72 + g * 8
                    value = picked[base:base + 8] + picked[base + 24:base + 32] + picked[base + 48:base + 56]
                    total = jnp.where(high_part == g, value, total)
                found[s].append(total)
        for s in range(2):
            stacked = jnp.stack(found[s], axis=0)
            bias_ref[s * 8:(s + 1) * 8, pl.ds(pl.multiple_of(step * 8, 8), 8), :] = jnp.transpose(stacked, (1, 0, 2))
        return carry

    lax.fori_loop(0, 6, some_rows, 0)
    for copy in first:
        copy.wait()

    def share(part, copies, n, target):
        copies.append(send(part, part, w_send.at[n], w_recv.at[n], target))

    third, fourth, fifth = [], [], []
    for d in range(3):
        share(other_ref.at[0:2, x, y, core], third, 3 + d, along_x[d])
        share(other_ref.at[2:4, x, y, core], third, 6 + d, along_y[d])
    lax.fori_loop(6, WT // 8, some_rows, 0)
    for h in range(16):
        bias_ref[h] = bias_ref[h] + blocked

    for copy in third + pieces:
        copy.wait()
    for d in range(3):
        share(other_ref.at[0:2, :, y, core], fourth, 9 + d, along_y[d])
        share(other_ref.at[2:4, x, :, core], fourth, 12 + d, along_x[d])
    share(other_ref.at[0:2, :, y, core], fifth, 15, sibling)
    share(other_ref.at[2:4, x, :, core], fifth, 16, sibling)

    def gather(which):
        halves = []
        for t in range(2):
            rows = held[t].reshape(2 * BOTH, 512)
            halves.append(jnp.dot(place_ref[which], rows, preferred_element_type=F32))
        return jnp.concatenate(halves, axis=1)

    cells = gather(0)
    center = jnp.mean(cells, axis=1, keepdims=True)
    cells = cells - center
    spread = jnp.mean(jnp.square(cells), axis=1, keepdims=True)
    inv_std = lax.rsqrt(spread + 1e-05)
    cells = cells * inv_std
    normed[...] = cells
    normed_bf[0:288] = cells.astype(BF)
    normed_bf[288:384] = jnp.zeros((96, 1024), BF)
    inv[...] = jnp.broadcast_to(inv_std, (288, 128))
    normed_t[...] = jnp.transpose(normed_bf[...], (1, 0)).reshape(32, 2, 16, 384)
    swaps = [send(normed_t.at[:, 1 - core], both_x.at[:, :, 384:768], t_send.at[1], t_recv.at[1], sibling)]
    grads[0:288] = gather(1).astype(BF)
    grads[288:384] = jnp.zeros((96, 1024), BF)
    grads_t[...] = jnp.transpose(grads[...], (1, 0)).reshape(32, 2, 16, 384)
    swaps.append(send(grads_t.at[:, 1 - core], both_g.at[:, :, 384:768], t_send.at[2], t_recv.at[2], sibling))
    both_x[:, :, 0:384] = normed_t[:, core]
    both_g[:, :, 0:384] = grads_t[:, core]

    for copy in own_weights:
        copy.wait()

    lane = lax.broadcasted_iota(jnp.int32, (WT, 128), 1)
    lower = lane < HD

    def split(value):
        zero = jnp.zeros_like(value)
        return jnp.concatenate([jnp.where(lower, value, zero), jnp.where(lower, zero, value)], axis=0)

    def weight(half, c):
        if half == 0:
            return (wq_ref[c] if c < 3 else wp_ref[...]).reshape(1024, 512)
        return other_ref[c].reshape(1024, 512)

    def project(half):
        for c in range(4):
            left = normed_bf if c < 3 else grads
            value = jnp.dot(left[0:288], weight(half, c), preferred_element_type=F32)
            value = value.astype(BF)
            if c == 0:
                value = value * jnp.asarray(0.125, BF)
            parts[c] = value

    def attend(half, start, stop):
        def pair(p, carry):
            span = pl.ds(pl.multiple_of(p * 128, 128), 128)
            for w in range(2):
                rows = pl.ds(w * WT, WT)
                q, k, v, g = (parts[c, rows, span] for c in range(4))
                qq, gg = split(q), split(g)
                bias = jnp.concatenate([bias_ref[half * 8 + 2 * p], bias_ref[half * 8 + 2 * p + 1]], axis=0)
                contract = (((1,), (1,)), ((), ()))
                flip = (((0,), (0,)), ((), ()))
                scores = lax.dot_general(qq, k, contract, preferred_element_type=F32) + bias
                weights = jnp.exp(scores)
                probs = weights / jnp.sum(weights, axis=1, keepdims=True)
                probs_bf = probs.astype(BF)
                found = jnp.dot(probs_bf, v, preferred_element_type=F32)
                dparts[half, 3, rows, span] = jnp.where(lower, found[0:WT], found[WT:]).astype(BF)
                gprobs = lax.dot_general(gg, v, contract, preferred_element_type=F32)
                dot_sum = jnp.sum(probs * gprobs, axis=1, keepdims=True)
                gscores = (probs * (gprobs - dot_sum)).astype(BF)
                gq = jnp.dot(gscores, k, preferred_element_type=F32)
                dparts[half, 0, rows, span] = (jnp.where(lower, gq[0:WT], gq[WT:]) * 0.125).astype(BF)
                dparts[half, 1, rows, span] = lax.dot_general(gscores, qq, flip, preferred_element_type=F32).astype(BF)
                dparts[half, 2, rows, span] = lax.dot_general(probs_bf, gg, flip, preferred_element_type=F32).astype(BF)
            return carry

        lax.fori_loop(start, stop, pair, 0)

    def input_grad(half):
        for c in range(3):
            value = lax.dot_general(dparts[half, c, 0:288], weight(half, c), (((1,), (1,)), ((), ())), preferred_element_type=F32)
            if half == 0 and c == 0:
                dx[...] = value
            else:
                dx[...] += value

    def swap(group, half, start, width):
        span = pl.ds(start, width)
        return send(dparts.at[half, :, 0:288, span], dparts.at[half, :, 384:672, span],
                    r_send.at[group, 0], r_recv.at[group, 0], sibling)

    def weight_grad(group, half, start, width, copy):
        mine, first_x, first_y = groups[group][0:3]
        span = pl.ds(start, width)
        copy.wait()
        stage = []
        for c in range(4):
            left = both_x if c < 3 else both_g
            value = jnp.dot(left[...].reshape(512, 768), dparts[half, c, :, span], preferred_element_type=F32)
            mine[c] = value.astype(BF).reshape(4, 2, 4, 16, width)
            for d in range(3):
                n = 4 + 3 * c + d
                if c % 2 == 0:
                    stage.append(send(mine.at[c, (x + d + 1) % 4], first_x.at[c // 2, d],
                                      r_send.at[group, n], r_recv.at[group, n], along_x[d]))
                else:
                    stage.append(send(mine.at[c, :, :, (y + d + 1) % 4], first_y.at[c // 2, d],
                                      r_send.at[group, n], r_recv.at[group, n], along_y[d]))
        return stage

    def reduce_second(group, copies):
        mine, first_x, first_y, mid_x, mid_y, second_x, second_y = groups[group][0:7]
        for copy in copies:
            copy.wait()
        for n in range(2):
            value = mine[2 * n, x].astype(F32)
            for d in range(3):
                value += first_x[n, d].astype(F32)
            mid_x[n] = value.astype(BF)
            value = mine[2 * n + 1, :, :, y].astype(F32)
            for d in range(3):
                value += first_y[n, d].astype(F32)
            mid_y[n] = value.astype(BF)
        stage = []
        for d in range(3):
            stage.append(send(mid_x.at[:, :, (y + d + 1) % 4], second_x.at[d],
                              r_send.at[group, 16 + d], r_recv.at[group, 16 + d], along_y[d]))
            stage.append(send(mid_y.at[:, (x + d + 1) % 4], second_y.at[d],
                              r_send.at[group, 19 + d], r_recv.at[group, 19 + d], along_x[d]))
        return stage

    def reduce_third(group, copies):
        mid_x, mid_y, second_x, second_y, z_out, z_in = groups[group][3:9]
        for copy in copies:
            copy.wait()
        for n in range(2):
            value = mid_x[n, :, y].astype(F32)
            for d in range(3):
                value += second_x[d, n].astype(F32)
            z_out[2 * n] = value.astype(BF)
            value = mid_y[n, x].astype(F32)
            for d in range(3):
                value += second_y[d, n].astype(F32)
            z_out[2 * n + 1] = value.astype(BF)
        return [send(z_out.at[:, 1 - zl], z_in, r_send.at[group, 22], r_recv.at[group, 22], along_z)]

    def reduced(group, c):
        z_out, z_in = groups[group][7:9]
        return z_out[c, zl].astype(F32) + z_in[c].astype(F32)

    project(0)
    attend(0, 0, 4)
    step = swap(0, 0, 0, 512)
    input_grad(0)
    for copy in swaps:
        copy.wait()
    stage0 = weight_grad(0, 0, 0, 512, step)
    for copy in fourth:
        copy.wait()
    for d in range(3):
        share(other_ref.at[0:2, :, (y + 3 - d) % 4, core], fifth, 17 + d, sibling)
        share(other_ref.at[2:4, (x + 3 - d) % 4, :, core], fifth, 20 + d, sibling)
    for copy in fifth:
        copy.wait()
    project(1)
    attend(1, 0, 2)
    step = swap(1, 1, 0, 256)
    stage0 = reduce_second(0, stage0)
    stage1 = weight_grad(1, 1, 0, 256, step)
    attend(1, 2, 4)
    step = swap(2, 1, 256, 256)
    stage0 = reduce_third(0, stage0)
    stage2 = weight_grad(2, 1, 256, 256, step)
    input_grad(1)

    total = dx[...]
    mean_grad = jnp.mean(total, axis=1, keepdims=True)
    mean_cross = jnp.mean(total * normed[...], axis=1, keepdims=True)
    result = (inv[:, 0:1] * (total - mean_grad - normed[...] * mean_cross)).astype(BF)
    moved = jnp.dot(placet_ref[...], result, preferred_element_type=F32).astype(BF)
    for di in range(2):
        for t in range(2):
            back[t, di] = moved[di * PIECE:(di + 1) * PIECE, t * 512:(t + 1) * 512]

    spans = (pl.ds(0, BIG), pl.ds(BIG, SMALL))
    pieces = []
    for n, (di, dj, to_tp, target) in enumerate(behind):
        pieces.append(send(back.at[to_tp, di, spans[dj]], landed.at[tp, di, spans[dj]],
                           back_send.at[n], back_recv.at[n], target))
    own = pltpu.make_async_copy(back.at[tp, 0, spans[0]], landed.at[tp, 0, spans[0]], local_sem.at[3])
    own.start()
    pieces.append(own)
    stage1 = reduce_second(1, stage1)
    stage2 = reduce_second(2, stage2)
    stage1 = reduce_third(1, stage1)
    stage2 = reduce_third(2, stage2)
    for copy in stage0 + stage1 + stage2:
        copy.wait()
    for c in range(4):
        t_out[c, :, 0:256] = reduced(1, c).astype(BF)
        t_out[c, :, 256:512] = reduced(2, c).astype(BF)
    last = send(t_out, t_in, t_send.at[0], t_recv.at[0], partner)
    for copy in pieces:
        copy.wait()
    last.wait()
    for c in range(4):
        total_ref[c] = reduced(0, c) + t_in[c].astype(F32)


def group_scratch(width):
    shapes = ((4, 4, 2, 4), (2, 3, 2, 4), (2, 3, 4, 2), (2, 2, 4), (2, 4, 2), (3, 2, 2), (3, 2, 2),
              (4, 2), (4,))
    return [pltpu.VMEM(shape + (16, width), BF) for shape in shapes]


def finish_kernel(landed, total_ref, packt_ref, tokens_ref, qkv_ref, proj_ref):
    for t in range(2):
        cells = landed[t].reshape(2 * PIECE, 512)
        moved = jnp.dot(packt_ref[...], cells, preferred_element_type=F32).astype(BF)
        if t == 0:
            tokens_ref[144:432, :] = moved
        else:
            tokens_ref[432:576, :] = moved[0:144]
            tokens_ref[0:144, :] = moved[144:288]
    qkv_ref[...] = total_ref[0:3]
    proj_ref[...] = total_ref[3]


VM = pl.BlockSpec(memory_space=pltpu.VMEM)
HB = pl.BlockSpec(memory_space=pl.ANY)
LIMIT = 60 * 1024 * 1024


def shards(tokens, w_qkv, w_proj, bias_table, bias_index, regions, out_grad):
    flat_in = tokens.reshape(576, 512)
    flat_grad = out_grad.reshape(576, 512)
    wq = w_qkv.transpose(1, 0, 2).reshape(3, 32, 32, 512)
    wp = w_proj.reshape(32, 32, 512)
    pack = jnp.asarray(PACK, BF)
    packt = jnp.asarray(UNPACK, BF)
    place = jnp.asarray(PLACE, BF)
    placet = jnp.asarray(LEAVE, BF)
    dma = pltpu.SemaphoreType.DMA
    shape = jax.ShapeDtypeStruct
    vmem = pltpu.VMEM
    landed, total = pl.pallas_call(
        whole_kernel,
        out_shape=(shape((2, 2, PIECE, 512), BF), shape((4, 16, 512), F32)),
        in_specs=[VM] * 5 + [HB] * 2 + [VM] * 3,
        out_specs=(VM, VM),
        scratch_shapes=[
            vmem((3, 32, 32, 512), BF), vmem((32, 32, 512), BF),
            vmem((4, 4, 4, 2, 32, 512), BF), vmem((2, 8, 768), F32),
            vmem((2, 2, BOTH, 512), BF), vmem((2, 2, BOTH, 512), BF), vmem((16, WT, WT), F32),
            vmem((288, 1024), F32), vmem((384, 1024), BF), vmem((384, 1024), BF),
            vmem((32, 2, 16, 384), BF), vmem((32, 2, 16, 384), BF), vmem((32, 16, 768), BF), vmem((32, 16, 768), BF),
            vmem((288, 128), F32), vmem((4, 288, 512), BF), vmem((2, 4, 768, 512), BF),
            vmem((288, 1024), F32), vmem((2, 2, PIECE, 512), BF),
            *group_scratch(512), *group_scratch(256), *group_scratch(256),
            vmem((4, 16, 512), BF), vmem((4, 16, 512), BF),
            dma((7,)), dma((7,)), dma((7,)), dma((7,)), dma((23,)), dma((23,)), dma((3, 23)), dma((3, 23)), dma((3,)), dma((3,)), dma((4,)),
        ],
        compiler_params=pltpu.CompilerParams(collective_id=0, has_side_effects=True, vmem_limit_bytes=LIMIT),
        name="whole",
    )(flat_in, flat_grad, pack, place, placet, wq, wp, bias_table.T, bias_index, regions.transpose(1, 0, 2))

    grad_tokens, qkv_grad, proj_grad = pl.pallas_call(
        finish_kernel,
        out_shape=(shape((576, 512), BF), shape((3, 16, 512), F32), shape((16, 512), F32)),
        in_specs=[VM] * 3,
        out_specs=(VM, VM, VM),
        name="finish",
    )(landed, total, packt)
    return grad_tokens.reshape(tokens.shape), qkv_grad.transpose(1, 0, 2), proj_grad


def solution(mesh):
    in_specs = (
        P(None, "lat", "lon", "tp"),
        P(None, None, "tp"),
        P(None, "tp"),
        P(None, "tp"),
        P(),
        P(None, "lat", "lon"),
        P(None, "lat", "lon", "tp"),
    )
    out_specs = (
        P(None, "lat", "lon", "tp"),
        P(("lat", "lon"), None, "tp"),
        P(("lat", "lon"), "tp"),
    )
    return jax.shard_map(shards, mesh=mesh, in_specs=in_specs, out_specs=out_specs, check_vma=False)
```

```python
import functools

import jax
import jax.numpy as jnp
import numpy as np
from jax import lax
from jax.experimental import pallas as pl
from jax.experimental.pallas import tpu as pltpu
from jax.sharding import PartitionSpec as P

HD = 64
WT = 144
BIG = 112
SMALL = 48
PIECE = BIG + SMALL
BOTH_BIG = 224
BOTH_SMALL = 80
BOTH = BOTH_BIG + BOTH_SMALL
MESH = pl.DeviceIdType.MESH
BF = jnp.bfloat16
F32 = jnp.float32
FAR = -1e30


def permutations():
    pack = np.zeros((2, BOTH, 576), np.float32)
    place = np.zeros((2, 288, 2 * BOTH), np.float32)
    leave = np.zeros((2 * PIECE, 288), np.float32)
    unpack = np.zeros((288, 2 * PIECE), np.float32)
    for di in range(2):
        for lv in range(2):
            for row in range(3):
                local = row + (3 if di == 0 else 0)
                for col in range(24):
                    cell = lv * 144 + local * 24 + col
                    shifted = (col - 6) % 24
                    window = (shifted // 12) * 144 + lv * 72 + (row + 3 * di) * 12 + shifted % 12
                    big = lv * 54 + row * 18 + col - 6
                    small = lv * 18 + row * 6 + col
                    for which in range(2):
                        spot = which * 108 + big if col >= 6 else BOTH_BIG + which * 36 + small
                        pack[di, spot, which * 288 + cell] = 1
                        place[which, window, di * BOTH + spot] = 1
                    spot = big if col >= 6 else BIG + small
                    leave[di * PIECE + spot, window] = 1
                    unpack[cell, di * PIECE + spot] = 1
    return pack, place, leave, unpack


PACK, PLACE, LEAVE, UNPACK = permutations()


def position():
    lat, lon, tp = lax.axis_index("lat"), lax.axis_index("lon"), lax.axis_index("tp")
    return lat, lon, tp


def device(lat, lon, tp):
    return {"lat": lat, "lon": lon, "tp": tp}


def neighbours():
    lat, lon, tp = position()
    x, zl, y, core = lat // 2, lat % 2, lon // 2, lon % 2
    sibling = device(lat, y * 2 + 1 - core, tp)
    along_x = [device(((x + d) % 4) * 2 + zl, lon, tp) for d in (1, 2, 3)]
    along_y = [device(lat, ((y + d) % 4) * 2 + core, tp) for d in (1, 2, 3)]
    along_z = device(x * 2 + 1 - zl, lon, tp)
    partner = device(lat, lon, 1 - tp)
    return x, zl, y, core, sibling, along_x, along_y, along_z, partner


def piece_ends(sign):
    lat, lon, tp = position()
    ends = []
    for di in range(2):
        for dj in range(2):
            for other in range(2):
                if di == 0 and dj == 0 and other == 0:
                    continue
                to_tp = 1 - tp if other else tp
                ends.append((di, dj, to_tp, device((lat + sign * di + 8) % 8, (lon + sign * dj + 8) % 8, to_tp)))
    return ends


def send(src, dst, send_sem, recv_sem, target):
    copy = pltpu.make_async_remote_copy(
        src_ref=src, dst_ref=dst, send_sem=send_sem, recv_sem=recv_sem, device_id=target, device_id_type=MESH
    )
    copy.start()
    return copy


def whole_kernel(tok_ref, grad_ref, pack_ref, place_ref, placet_ref, wq_hbm, wp_hbm, table_ref, index_ref, regions_ref,
                 landed, total_ref,
                 wq_ref, wp_ref, other_ref, tables_ref, packed, held, bias_ref,
                 normed, normed_bf, grads, normed_t, grads_t, both_x, both_g, inv, parts, dparts, dx, back,
                 *rest):
    groups, sems = (rest[0:18], rest[18:27], rest[27:36]), rest[36:]
    (piece_send, piece_recv, back_send, back_recv, w_send, w_recv, r_send, r_recv, t_send, t_recv, local_sem) = sems
    lat, lon, tp = position()
    x, zl, y, core, sibling, along_x, along_y, along_z, partner = neighbours()
    ahead, behind = piece_ends(-1), piece_ends(1)
    barrier = pltpu.get_barrier_semaphore()
    diagonal = device(x * 2 + 1 - zl, lon, 1 - tp)
    targets = [diagonal] + [e[3] for e in ahead] + [e[3] for e in behind] + [sibling, along_z, partner] + along_x + along_y
    for target in targets:
        pl.semaphore_signal(barrier, inc=1, device_id=target, device_id_type=MESH)

    own_weights = [
        pltpu.make_async_copy(wq_hbm, wq_ref, local_sem.at[0]),
        pltpu.make_async_copy(wp_hbm, wp_ref, local_sem.at[1]),
    ]
    for copy in own_weights:
        copy.start()

    tables_ref[0] = jnp.zeros((8, 768), F32)
    tables_ref[0, :, 0:759] = table_ref[...]

    def pack(half):
        cells = []
        for ref in (tok_ref, grad_ref):
            if half == 0:
                cells.append(ref[144:432, :])
            else:
                cells.extend([ref[432:576, :], ref[0:144, :]])
        cells = jnp.concatenate(cells, axis=0)
        for di in range(2):
            packed[half, di] = jnp.dot(pack_ref[di], cells, preferred_element_type=F32).astype(BF)

    pl.semaphore_wait(barrier, len(targets))

    mine = (x * 4 + y) * 2 + core
    first = [
        send(wq_hbm.at[:, mine], other_ref.at[0:3, x, y, core], w_send.at[0], w_recv.at[0], partner),
        send(wp_hbm.at[mine], other_ref.at[3, x, y, core], w_send.at[1], w_recv.at[1], partner),
        send(tables_ref.at[0], tables_ref.at[1], w_send.at[2], w_recv.at[2], partner),
    ]
    spans = (pl.ds(0, BOTH_BIG), pl.ds(BOTH_BIG, BOTH_SMALL))
    pack(0)
    pack(1)
    pieces = []
    for n, (di, dj, to_tp, target) in enumerate(ahead):
        pieces.append(send(packed.at[to_tp, di, spans[dj]], held.at[tp, di, spans[dj]],
                           piece_send.at[n], piece_recv.at[n], target))
    own = pltpu.make_async_copy(packed.at[tp, 0, spans[0]], held.at[tp, 0, spans[0]], local_sem.at[2])
    own.start()
    pieces.append(own)

    for half in range(2):
        for c in range(4):
            for base in (288, 672):
                dparts[half, c, base:base + 96] = jnp.zeros((96, 512), BF)

    rows = lax.broadcasted_iota(jnp.int32, (WT, WT), 0) // 12
    cols = lax.broadcasted_iota(jnp.int32, (WT, WT), 1) // 12
    left = jnp.zeros((WT, WT), jnp.int32)
    right = jnp.zeros((WT, WT), jnp.int32)
    for lv in range(2):
        for row in range(6):
            value = regions_ref[row, pl.ds(2 * tp + lv, 1), 0:1]
            left = jnp.where(rows == lv * 6 + row, value, left)
            right = jnp.where(cols == lv * 6 + row, value, right)
    blocked = jnp.where(left == right, 0.0, FAR).astype(F32)

    first.pop().wait()
    blocks = []
    for s in range(2):
        table = tables_ref[s]
        top = table.astype(BF).astype(F32)
        rest = table - top
        mid = rest.astype(BF).astype(F32)
        low = rest - mid
        for part in (top, mid, low):
            for g in range(3):
                blocks.append(part[:, g * 256:(g + 1) * 256])
    matrix = jnp.concatenate(blocks, axis=0).astype(BF)
    depth = lax.broadcasted_iota(jnp.int32, (256, WT), 0)

    def some_rows(step, carry):
        found = ([], [])
        index = index_ref[pl.ds(pl.multiple_of(step * 8, 8), 8), :]
        for r in range(8):
            row = index[r:r + 1, :]
            low_part, high_part = row & 255, row >> 8
            hot = jnp.where(depth == low_part, 1.0, 0.0).astype(BF)
            picked = jnp.dot(matrix, hot, preferred_element_type=F32)
            for s in range(2):
                total = jnp.zeros((8, WT), F32)
                for g in range(3):
                    base = s * 72 + g * 8
                    value = picked[base:base + 8] + picked[base + 24:base + 32] + picked[base + 48:base + 56]
                    total = jnp.where(high_part == g, value, total)
                found[s].append(total)
        for s in range(2):
            stacked = jnp.stack(found[s], axis=0)
            bias_ref[s * 8:(s + 1) * 8, pl.ds(pl.multiple_of(step * 8, 8), 8), :] = jnp.transpose(stacked, (1, 0, 2))
        return carry

    lax.fori_loop(0, 4, some_rows, 0)
    for copy in first:
        copy.wait()

    def share(part, copies, n, target):
        copies.append(send(part, part, w_send.at[n], w_recv.at[n], target))

    third, fourth, fifth = [], [], []
    for d in range(3):
        share(other_ref.at[0:2, x, y, core], third, 3 + d, along_y[d])
        share(other_ref.at[2:4, x, y, core], third, 6 + d, along_x[d])
    lax.fori_loop(4, 10, some_rows, 0)
    lax.fori_loop(10, WT // 8, some_rows, 0)
    for h in range(16):
        bias_ref[h] = bias_ref[h] + blocked

    for copy in third + pieces:
        copy.wait()
    for d in (0, 2):
        share(other_ref.at[0:2, x, :, core], fourth, 9 + d, along_x[d])
        share(other_ref.at[2:4, :, y, core], fourth, 12 + d, along_y[d])
    share(other_ref.at[0:2, x, :, core], fifth, 15, sibling)
    share(other_ref.at[2:4, :, y, core], fifth, 16, sibling)

    def gather(which):
        halves = []
        for t in range(2):
            rows = held[t].reshape(2 * BOTH, 512)
            halves.append(jnp.dot(place_ref[which], rows, preferred_element_type=F32))
        return jnp.concatenate(halves, axis=1)

    cells = gather(0)
    center = jnp.mean(cells, axis=1, keepdims=True)
    cells = cells - center
    spread = jnp.mean(jnp.square(cells), axis=1, keepdims=True)
    inv_std = lax.rsqrt(spread + 1e-05)
    cells = cells * inv_std
    normed[...] = cells
    normed_bf[0:288] = cells.astype(BF)
    normed_bf[288:384] = jnp.zeros((96, 1024), BF)
    inv[...] = jnp.broadcast_to(inv_std, (288, 128))
    normed_t[...] = jnp.transpose(normed_bf[...], (1, 0)).reshape(32, 2, 16, 384)
    swaps = [send(normed_t.at[:, 1 - core], both_x.at[:, :, 384:768], t_send.at[1], t_recv.at[1], sibling)]
    grads[0:288] = gather(1).astype(BF)
    grads[288:384] = jnp.zeros((96, 1024), BF)
    grads_t[...] = jnp.transpose(grads[...], (1, 0)).reshape(32, 2, 16, 384)
    swaps.append(send(grads_t.at[:, 1 - core], both_g.at[:, :, 384:768], t_send.at[2], t_recv.at[2], sibling))
    both_x[:, :, 0:384] = normed_t[:, core]
    both_g[:, :, 0:384] = grads_t[:, core]

    for copy in own_weights:
        copy.wait()

    lane = lax.broadcasted_iota(jnp.int32, (WT, 128), 1)
    lower = lane < HD

    def split(value):
        zero = jnp.zeros_like(value)
        return jnp.concatenate([jnp.where(lower, value, zero), jnp.where(lower, zero, value)], axis=0)

    def weight(half, c):
        if half == 0:
            return (wq_ref[c] if c < 3 else wp_ref[...]).reshape(1024, 512)
        return other_ref[c].reshape(1024, 512)

    def project(half):
        for c in range(4):
            left = normed_bf if c < 3 else grads
            value = jnp.dot(left[0:288], weight(half, c), preferred_element_type=F32)
            value = value.astype(BF)
            if c == 0:
                value = value * jnp.asarray(0.125, BF)
            parts[c] = value

    def attend(half, start, stop):
        def pair(p, carry):
            span = pl.ds(pl.multiple_of(p * 128, 128), 128)
            for w in range(2):
                rows = pl.ds(w * WT, WT)
                q, k, v, g = (parts[c, rows, span] for c in range(4))
                qq, gg = split(q), split(g)
                bias = jnp.concatenate([bias_ref[half * 8 + 2 * p], bias_ref[half * 8 + 2 * p + 1]], axis=0)
                contract = (((1,), (1,)), ((), ()))
                flip = (((0,), (0,)), ((), ()))
                scores = lax.dot_general(qq, k, contract, preferred_element_type=F32) + bias
                weights = jnp.exp(scores)
                probs = weights / jnp.sum(weights, axis=1, keepdims=True)
                probs_bf = probs.astype(BF)
                found = jnp.dot(probs_bf, v, preferred_element_type=F32)
                dparts[half, 3, rows, span] = jnp.where(lower, found[0:WT], found[WT:]).astype(BF)
                gprobs = lax.dot_general(gg, v, contract, preferred_element_type=F32)
                dot_sum = jnp.sum(probs * gprobs, axis=1, keepdims=True)
                gscores = (probs * (gprobs - dot_sum)).astype(BF)
                gq = jnp.dot(gscores, k, preferred_element_type=F32)
                dparts[half, 0, rows, span] = (jnp.where(lower, gq[0:WT], gq[WT:]) * 0.125).astype(BF)
                dparts[half, 1, rows, span] = lax.dot_general(gscores, qq, flip, preferred_element_type=F32).astype(BF)
                dparts[half, 2, rows, span] = lax.dot_general(probs_bf, gg, flip, preferred_element_type=F32).astype(BF)
            return carry

        lax.fori_loop(start, stop, pair, 0)

    def input_grad(half):
        for c in range(3):
            value = lax.dot_general(dparts[half, c, 0:288], weight(half, c), (((1,), (1,)), ((), ())), preferred_element_type=F32)
            if half == 0 and c == 0:
                dx[...] = value
            else:
                dx[...] += value

    def swap(group, half, start, width):
        span = pl.ds(start, width)
        return send(dparts.at[half, :, 0:288, span], dparts.at[half, :, 384:672, span],
                    r_send.at[group, 0], r_recv.at[group, 0], sibling)

    def weight_grad(group, half, start, width, copy):
        mine, first_x, first_y = groups[group][0:3]
        span = pl.ds(start, width)
        copy.wait()
        stage = []
        for c in range(4):
            left = both_x if c < 3 else both_g
            value = jnp.dot(left[...].reshape(512, 768), dparts[half, c, :, span], preferred_element_type=F32)
            mine[c] = value.astype(BF).reshape(4, 2, 4, 16, width)
            for d in range(3):
                n = 1 + 3 * c + d
                if c % 2 == 0:
                    stage.append(send(mine.at[c, (x + d + 1) % 4], first_x.at[c // 2, d],
                                      r_send.at[group, n], r_recv.at[group, n], along_x[d]))
                else:
                    stage.append(send(mine.at[c, :, :, (y + d + 1) % 4], first_y.at[c // 2, d],
                                      r_send.at[group, n], r_recv.at[group, n], along_y[d]))
        return stage

    def plus(value, others):
        value = value.astype(F32)
        for d in range(3):
            value += others[d].astype(F32)
        return value

    def reduce_second(group, copies):
        mine, first_x, first_y, mid_x, mid_y, second_x, second_y = groups[group][0:7]
        for copy in copies:
            copy.wait()
        for n in range(2):
            mid_x[n] = plus(mine[2 * n, x], first_x[n]).astype(BF)
            mid_y[n] = plus(mine[2 * n + 1, :, :, y], first_y[n]).astype(BF)
        stage = []
        for d in range(3):
            stage.append(send(mid_x.at[:, :, (y + d + 1) % 4], second_x.at[d],
                              r_send.at[group, 13 + d], r_recv.at[group, 13 + d], along_y[d]))
            stage.append(send(mid_y.at[:, (x + d + 1) % 4], second_y.at[d],
                              r_send.at[group, 16 + d], r_recv.at[group, 16 + d], along_x[d]))
        return stage

    def reduce_third(group, copies):
        mid_x, mid_y, second_x, second_y, z_out, z_in = groups[group][3:9]
        for copy in copies:
            copy.wait()
        for n in range(2):
            z_out[2 * n] = plus(mid_x[n, :, y], [second_x[d, n] for d in range(3)]).astype(BF)
            z_out[2 * n + 1] = plus(mid_y[n, x], [second_y[d, n] for d in range(3)]).astype(BF)
        return [
            send(z_out.at[:, zl], z_in.at[0], r_send.at[group, 19], r_recv.at[group, 19], partner),
            send(z_out.at[:, 1 - zl], z_in.at[1], r_send.at[group, 20], r_recv.at[group, 20], diagonal),
        ]

    def early_grad(group, half, start, width, copy):
        mine, first_x, first_y, first_z = groups[group][0:4]
        span = pl.ds(start, width)
        copy.wait()
        stage = []
        for c in (2, 3, 0, 1):
            left = both_x if c < 3 else both_g
            value = jnp.dot(left[...].reshape(512, 768), dparts[half, c, :, span], preferred_element_type=F32)
            mine[c] = value.astype(BF).reshape(4, 2, 4, 16, width)
            if c == 3:
                stage.append(send(mine.at[2:4, :, 1 - zl], first_z, r_send.at[group, 1], r_recv.at[group, 1], along_z))
            for d in range(3):
                if c == 0:
                    stage.append(send(mine.at[0, (x + d + 1) % 4], first_x.at[d],
                                      r_send.at[group, 2 + d], r_recv.at[group, 2 + d], along_x[d]))
                if c == 1:
                    stage.append(send(mine.at[1, :, :, (y + d + 1) % 4], first_y.at[d],
                                      r_send.at[group, 5 + d], r_recv.at[group, 5 + d], along_y[d]))
        return stage

    def early_second(group, copies):
        mine, first_x, first_y, first_z, mid_x, mid_y, mid_z, second_x, second_y, second_zx, second_zy = groups[group][0:11]
        for copy in copies:
            copy.wait()
        mid_x[...] = plus(mine[0, x], first_x).astype(BF)
        mid_y[...] = plus(mine[1, :, :, y], first_y).astype(BF)
        mid_z[...] = (mine[2:4, :, zl].astype(F32) + first_z[...].astype(F32)).astype(BF)
        stage = []
        for d in range(3):
            to_x, to_y = (x + d + 1) % 4, (y + d + 1) % 4
            for n, (src, dst, target) in enumerate((
                (mid_z.at[0, to_x], second_zx.at[d], along_x[d]),
                (mid_z.at[1, :, to_y], second_zy.at[d], along_y[d]),
                (mid_x.at[:, to_y], second_x.at[d], along_y[d]),
                (mid_y.at[to_x], second_y.at[d], along_x[d]),
            )):
                stage.append(send(src, dst, r_send.at[group, 8 + 4 * d + n], r_recv.at[group, 8 + 4 * d + n], target))
        return stage

    def early_third(group, copies):
        (mid_x, mid_y, mid_z, second_x, second_y, second_zx, second_zy, z_out, z_in,
         late_x, late_y, third_x, third_y) = groups[group][4:17]
        for copy in copies:
            copy.wait()
        z_out[0] = plus(mid_x[:, y], second_x).astype(BF)
        z_out[1] = plus(mid_y[x], second_y).astype(BF)
        late_x[...] = plus(mid_z[0, x], second_zx).astype(BF)
        late_y[...] = plus(mid_z[1, :, y], second_zy).astype(BF)
        stage = [send(z_out.at[:, 1 - zl], z_in, r_send.at[group, 20], r_recv.at[group, 20], along_z)]
        for d in range(3):
            stage.append(send(late_x.at[(y + d + 1) % 4], third_x.at[d],
                              r_send.at[group, 21 + d], r_recv.at[group, 21 + d], along_y[d]))
            stage.append(send(late_y.at[(x + d + 1) % 4], third_y.at[d],
                              r_send.at[group, 24 + d], r_recv.at[group, 24 + d], along_x[d]))
        return stage

    def early_last(group, copies):
        z_out, z_in, late_x, late_y, third_x, third_y, done = groups[group][11:18]
        for copy in copies:
            copy.wait()
        for c in range(2):
            done[c] = z_out[c, zl].astype(F32) + z_in[c].astype(F32)
        done[2] = plus(late_x[y], third_x)
        done[3] = plus(late_y[x], third_y)

    project(0)
    attend(0, 0, 2)
    for copy in fourth:
        copy.wait()
    relay = []
    for d in (0, 2):
        from_y, from_x = (y + 3 - d) % 4, (x + 3 - d) % 4
        part = pl.ds(d, 2)
        share(other_ref.at[0:2, from_x, part, core], relay, 23 + d, along_x[d])
        share(other_ref.at[2:4, part, from_y, core], relay, 24 + d, along_y[d])
        share(other_ref.at[0:2, from_x, :, core], fifth, 17 + d, sibling)
        share(other_ref.at[2:4, :, from_y, core], fifth, 20 + d, sibling)
    attend(0, 2, 4)
    step = swap(0, 0, 0, 512)
    input_grad(0)
    for copy in swaps + relay:
        copy.wait()
    share(other_ref.at[0:2, (x + 2) % 4, :, core], fifth, 18, sibling)
    share(other_ref.at[2:4, :, (y + 2) % 4, core], fifth, 21, sibling)
    stage0 = early_grad(0, 0, 0, 512, step)
    for copy in fifth:
        copy.wait()
    project(1)
    attend(1, 0, 3)
    step = swap(1, 1, 0, 384)
    stage1 = weight_grad(1, 1, 0, 384, step)
    stage0 = early_second(0, stage0)
    attend(1, 3, 4)
    step = swap(2, 1, 384, 128)
    stage2 = weight_grad(2, 1, 384, 128, step)
    stage0 = early_third(0, stage0)
    input_grad(1)

    total = dx[...]
    mean_grad = jnp.mean(total, axis=1, keepdims=True)
    mean_cross = jnp.mean(total * normed[...], axis=1, keepdims=True)
    result = (inv[:, 0:1] * (total - mean_grad - normed[...] * mean_cross)).astype(BF)
    moved = jnp.dot(placet_ref[...], result, preferred_element_type=F32).astype(BF)
    for di in range(2):
        for t in range(2):
            back[t, di] = moved[di * PIECE:(di + 1) * PIECE, t * 512:(t + 1) * 512]

    spans = (pl.ds(0, BIG), pl.ds(BIG, SMALL))
    pieces = []
    for n, (di, dj, to_tp, target) in enumerate(behind):
        pieces.append(send(back.at[to_tp, di, spans[dj]], landed.at[tp, di, spans[dj]],
                           back_send.at[n], back_recv.at[n], target))
    own = pltpu.make_async_copy(back.at[tp, 0, spans[0]], landed.at[tp, 0, spans[0]], local_sem.at[3])
    own.start()
    pieces.append(own)
    stage1 = reduce_second(1, stage1)
    stage2 = reduce_second(2, stage2)
    stage1 = reduce_third(1, stage1)
    early_last(0, stage0)
    stage2 = reduce_third(2, stage2)
    for copy in pieces + stage1 + stage2:
        copy.wait()
    done = groups[0][17]
    for group, span in ((1, pl.ds(0, 384)), (2, pl.ds(384, 128))):
        others = groups[group][8]
        total_ref[:, :, span] = (done[:, :, span] + others[0].astype(F32) + others[1].astype(F32))


def early_scratch(width):
    shapes = ((4, 4, 2, 4), (3, 2, 4), (3, 4, 2), (2, 4, 4), (2, 4), (4, 2), (2, 4, 4),
              (3, 2), (3, 2), (3, 4), (3, 4), (2, 2), (2,), (4,), (4,), (3,), (3,))
    return [pltpu.VMEM(shape + (16, width), BF) for shape in shapes] + [pltpu.VMEM((4, 16, width), F32)]


def group_scratch(width):
    shapes = ((4, 4, 2, 4), (2, 3, 2, 4), (2, 3, 4, 2), (2, 2, 4), (2, 4, 2), (3, 2, 2), (3, 2, 2), (4, 2), (2, 4))
    return [pltpu.VMEM(shape + (16, width), BF) for shape in shapes]


def finish_kernel(landed, total_ref, packt_ref, tokens_ref, qkv_ref, proj_ref):
    for t in range(2):
        cells = landed[t].reshape(2 * PIECE, 512)
        moved = jnp.dot(packt_ref[...], cells, preferred_element_type=F32).astype(BF)
        if t == 0:
            tokens_ref[144:432, :] = moved
        else:
            tokens_ref[432:576, :] = moved[0:144]
            tokens_ref[0:144, :] = moved[144:288]
    qkv_ref[...] = total_ref[0:3]
    proj_ref[...] = total_ref[3]


VM = pl.BlockSpec(memory_space=pltpu.VMEM)
HB = pl.BlockSpec(memory_space=pl.ANY)
LIMIT = 60 * 1024 * 1024


def shards(tokens, w_qkv, w_proj, bias_table, bias_index, regions, out_grad):
    flat_in = tokens.reshape(576, 512)
    flat_grad = out_grad.reshape(576, 512)
    wq = w_qkv.transpose(1, 0, 2).reshape(3, 32, 32, 512)
    wp = w_proj.reshape(32, 32, 512)
    pack = jnp.asarray(PACK, BF)
    packt = jnp.asarray(UNPACK, BF)
    place = jnp.asarray(PLACE, BF)
    placet = jnp.asarray(LEAVE, BF)
    dma = pltpu.SemaphoreType.DMA
    shape = jax.ShapeDtypeStruct
    vmem = pltpu.VMEM
    landed, total = pl.pallas_call(
        whole_kernel,
        out_shape=(shape((2, 2, PIECE, 512), BF), shape((4, 16, 512), F32)),
        in_specs=[VM] * 5 + [HB] * 2 + [VM] * 3,
        out_specs=(VM, VM),
        scratch_shapes=[
            vmem((3, 32, 32, 512), BF), vmem((32, 32, 512), BF),
            vmem((4, 4, 4, 2, 32, 512), BF), vmem((2, 8, 768), F32),
            vmem((2, 2, BOTH, 512), BF), vmem((2, 2, BOTH, 512), BF), vmem((16, WT, WT), F32),
            vmem((288, 1024), F32), vmem((384, 1024), BF), vmem((384, 1024), BF),
            vmem((32, 2, 16, 384), BF), vmem((32, 2, 16, 384), BF), vmem((32, 16, 768), BF), vmem((32, 16, 768), BF),
            vmem((288, 128), F32), vmem((4, 288, 512), BF), vmem((2, 4, 768, 512), BF),
            vmem((288, 1024), F32), vmem((2, 2, PIECE, 512), BF),
            *early_scratch(512), *group_scratch(384), *group_scratch(128),
            dma((7,)), dma((7,)), dma((7,)), dma((7,)), dma((27,)), dma((27,)), dma((3, 27)), dma((3, 27)), dma((3,)), dma((3,)), dma((4,)),
        ],
        compiler_params=pltpu.CompilerParams(collective_id=0, has_side_effects=True, vmem_limit_bytes=LIMIT),
        name="whole",
    )(flat_in, flat_grad, pack, place, placet, wq, wp, bias_table.T, bias_index, regions.transpose(1, 0, 2))

    grad_tokens, qkv_grad, proj_grad = pl.pallas_call(
        finish_kernel,
        out_shape=(shape((576, 512), BF), shape((3, 16, 512), F32), shape((16, 512), F32)),
        in_specs=[VM] * 3,
        out_specs=(VM, VM, VM),
        name="finish",
    )(landed, total, packt)
    return grad_tokens.reshape(tokens.shape), qkv_grad.transpose(1, 0, 2), proj_grad


def solution(mesh):
    in_specs = (
        P(None, "lat", "lon", "tp"),
        P(None, None, "tp"),
        P(None, "tp"),
        P(None, "tp"),
        P(),
        P(None, "lat", "lon"),
        P(None, "lat", "lon", "tp"),
    )
    out_specs = (
        P(None, "lat", "lon", "tp"),
        P(("lat", "lon"), None, "tp"),
        P(("lat", "lon"), "tp"),
    )
    return jax.shard_map(shards, mesh=mesh, in_specs=in_specs, out_specs=out_specs, check_vma=False)
```

```python
import functools

import jax
import jax.numpy as jnp
import numpy as np
from jax import lax
from jax.experimental import pallas as pl
from jax.experimental.pallas import tpu as pltpu
from jax.sharding import PartitionSpec as P

HD = 64
WT = 144
BIG = 112
SMALL = 48
PIECE = BIG + SMALL
BOTH_BIG = 224
BOTH_SMALL = 80
BOTH = BOTH_BIG + BOTH_SMALL
MESH = pl.DeviceIdType.MESH
BF = jnp.bfloat16
F32 = jnp.float32
FAR = -1e30


def permutations():
    pack = np.zeros((2, BOTH, 576), np.float32)
    place = np.zeros((2, 288, 2 * BOTH), np.float32)
    leave = np.zeros((2 * PIECE, 288), np.float32)
    unpack = np.zeros((288, 2 * PIECE), np.float32)
    for di in range(2):
        for lv in range(2):
            for row in range(3):
                local = row + (3 if di == 0 else 0)
                for col in range(24):
                    cell = lv * 144 + local * 24 + col
                    shifted = (col - 6) % 24
                    window = (shifted // 12) * 144 + lv * 72 + (row + 3 * di) * 12 + shifted % 12
                    big = lv * 54 + row * 18 + col - 6
                    small = lv * 18 + row * 6 + col
                    for which in range(2):
                        spot = which * 108 + big if col >= 6 else BOTH_BIG + which * 36 + small
                        pack[di, spot, which * 288 + cell] = 1
                        place[which, window, di * BOTH + spot] = 1
                    spot = big if col >= 6 else BIG + small
                    leave[di * PIECE + spot, window] = 1
                    unpack[cell, di * PIECE + spot] = 1
    return pack, place, leave, unpack


PACK, PLACE, LEAVE, UNPACK = permutations()


def position():
    lat, lon, tp = lax.axis_index("lat"), lax.axis_index("lon"), lax.axis_index("tp")
    return lat, lon, tp


def device(lat, lon, tp):
    return {"lat": lat, "lon": lon, "tp": tp}


def neighbours():
    lat, lon, tp = position()
    x, zl, y, core = lat // 2, lat % 2, lon // 2, lon % 2
    sibling = device(lat, y * 2 + 1 - core, tp)
    along_x = [device(((x + d) % 4) * 2 + zl, lon, tp) for d in (1, 2, 3)]
    along_y = [device(lat, ((y + d) % 4) * 2 + core, tp) for d in (1, 2, 3)]
    along_z = device(x * 2 + 1 - zl, lon, tp)
    partner = device(lat, lon, 1 - tp)
    return x, zl, y, core, sibling, along_x, along_y, along_z, partner


def piece_ends(sign):
    lat, lon, tp = position()
    ends = []
    for di in range(2):
        for dj in range(2):
            for other in range(2):
                if di == 0 and dj == 0 and other == 0:
                    continue
                to_tp = 1 - tp if other else tp
                ends.append((di, dj, to_tp, device((lat + sign * di + 8) % 8, (lon + sign * dj + 8) % 8, to_tp)))
    return ends


def send(src, dst, send_sem, recv_sem, target):
    copy = pltpu.make_async_remote_copy(
        src_ref=src, dst_ref=dst, send_sem=send_sem, recv_sem=recv_sem, device_id=target, device_id_type=MESH
    )
    copy.start()
    return copy


def whole_kernel(tok_ref, grad_ref, pack_ref, place_ref, placet_ref, wq_hbm, wp_hbm, table_ref, index_ref, regions_ref,
                 landed, total_ref,
                 wq_ref, wp_ref, other_ref, tables_ref, packed, held, bias_ref,
                 normed, normed_bf, grads, normed_t, grads_t, both_x, both_g, inv, parts, dparts, dx, back,
                 *rest):
    groups, sems = (rest[0:18], rest[18:27], rest[27:36]), rest[36:]
    (piece_send, piece_recv, back_send, back_recv, w_send, w_recv, r_send, r_recv, t_send, t_recv, local_sem) = sems
    lat, lon, tp = position()
    x, zl, y, core, sibling, along_x, along_y, along_z, partner = neighbours()
    ahead, behind = piece_ends(-1), piece_ends(1)
    barrier = pltpu.get_barrier_semaphore()
    diagonal = device(x * 2 + 1 - zl, lon, 1 - tp)
    targets = [diagonal] + [e[3] for e in ahead] + [e[3] for e in behind] + [sibling, along_z, partner] + along_x + along_y
    for target in targets:
        pl.semaphore_signal(barrier, inc=1, device_id=target, device_id_type=MESH)

    own_weights = [
        pltpu.make_async_copy(wq_hbm, wq_ref, local_sem.at[0]),
        pltpu.make_async_copy(wp_hbm, wp_ref, local_sem.at[1]),
    ]
    for copy in own_weights:
        copy.start()

    tables_ref[0] = jnp.zeros((8, 768), F32)
    tables_ref[0, :, 0:759] = table_ref[...]

    def pack(half):
        cells = []
        for ref in (tok_ref, grad_ref):
            if half == 0:
                cells.append(ref[144:432, :])
            else:
                cells.extend([ref[432:576, :], ref[0:144, :]])
        cells = jnp.concatenate(cells, axis=0)
        for di in range(2):
            packed[half, di] = jnp.dot(pack_ref[di], cells, preferred_element_type=F32).astype(BF)

    pl.semaphore_wait(barrier, len(targets))

    mine = (x * 4 + y) * 2 + core
    first = [
        send(wq_hbm.at[:, mine], other_ref.at[0:3, x, y, core], w_send.at[0], w_recv.at[0], partner),
        send(wp_hbm.at[mine], other_ref.at[3, x, y, core], w_send.at[1], w_recv.at[1], partner),
        send(tables_ref.at[0], tables_ref.at[1], w_send.at[2], w_recv.at[2], partner),
    ]
    spans = (pl.ds(0, BOTH_BIG), pl.ds(BOTH_BIG, BOTH_SMALL))
    pack(0)
    pack(1)
    pieces = []
    for n, (di, dj, to_tp, target) in enumerate(ahead):
        pieces.append(send(packed.at[to_tp, di, spans[dj]], held.at[tp, di, spans[dj]],
                           piece_send.at[n], piece_recv.at[n], target))
    own = pltpu.make_async_copy(packed.at[tp, 0, spans[0]], held.at[tp, 0, spans[0]], local_sem.at[2])
    own.start()
    pieces.append(own)

    for half in range(2):
        for c in range(4):
            for base in (288, 672):
                dparts[half, c, base:base + 96] = jnp.zeros((96, 512), BF)

    rows = lax.broadcasted_iota(jnp.int32, (WT, WT), 0) // 12
    cols = lax.broadcasted_iota(jnp.int32, (WT, WT), 1) // 12
    left = jnp.zeros((WT, WT), jnp.int32)
    right = jnp.zeros((WT, WT), jnp.int32)
    for lv in range(2):
        for row in range(6):
            value = regions_ref[row, pl.ds(2 * tp + lv, 1), 0:1]
            left = jnp.where(rows == lv * 6 + row, value, left)
            right = jnp.where(cols == lv * 6 + row, value, right)
    blocked = jnp.where(left == right, 0.0, FAR).astype(F32)

    first.pop().wait()
    blocks = []
    for s in range(2):
        table = tables_ref[s]
        top = table.astype(BF).astype(F32)
        rest = table - top
        mid = rest.astype(BF).astype(F32)
        low = rest - mid
        for part in (top, mid, low):
            for g in range(3):
                blocks.append(part[:, g * 256:(g + 1) * 256])
    matrix = jnp.concatenate(blocks, axis=0).astype(BF)
    depth = lax.broadcasted_iota(jnp.int32, (256, WT), 0)

    def some_rows(step, carry):
        found = ([], [])
        index = index_ref[pl.ds(pl.multiple_of(step * 8, 8), 8), :]
        for r in range(8):
            row = index[r:r + 1, :]
            low_part, high_part = row & 255, row >> 8
            hot = jnp.where(depth == low_part, 1.0, 0.0).astype(BF)
            picked = jnp.dot(matrix, hot, preferred_element_type=F32)
            for s in range(2):
                total = jnp.zeros((8, WT), F32)
                for g in range(3):
                    base = s * 72 + g * 8
                    value = picked[base:base + 8] + picked[base + 24:base + 32] + picked[base + 48:base + 56]
                    total = jnp.where(high_part == g, value, total)
                found[s].append(total)
        for s in range(2):
            stacked = jnp.stack(found[s], axis=0)
            bias_ref[s * 8:(s + 1) * 8, pl.ds(pl.multiple_of(step * 8, 8), 8), :] = jnp.transpose(stacked, (1, 0, 2))
        return carry

    lax.fori_loop(0, 4, some_rows, 0)
    for copy in first:
        copy.wait()

    def share(part, copies, n, target):
        copies.append(send(part, part, w_send.at[n], w_recv.at[n], target))

    third, fourth, fifth = [], [], []
    for d in range(3):
        share(other_ref.at[0:2, x, y, core], third, 3 + d, along_y[d])
        share(other_ref.at[2:4, x, y, core], third, 6 + d, along_x[d])
    lax.fori_loop(4, 10, some_rows, 0)
    lax.fori_loop(10, WT // 8, some_rows, 0)
    for h in range(16):
        bias_ref[h] = bias_ref[h] + blocked

    for copy in third + pieces:
        copy.wait()
    for d in (0, 2):
        share(other_ref.at[0:2, x, :, core], fourth, 9 + d, along_x[d])
        share(other_ref.at[2:4, :, y, core], fourth, 12 + d, along_y[d])
    share(other_ref.at[0:2, x, :, core], fifth, 15, sibling)
    share(other_ref.at[2:4, :, y, core], fifth, 16, sibling)

    def gather(which):
        halves = []
        for t in range(2):
            rows = held[t].reshape(2 * BOTH, 512)
            halves.append(jnp.dot(place_ref[which], rows, preferred_element_type=F32))
        return jnp.concatenate(halves, axis=1)

    cells = gather(0)
    center = jnp.mean(cells, axis=1, keepdims=True)
    cells = cells - center
    spread = jnp.mean(jnp.square(cells), axis=1, keepdims=True)
    inv_std = lax.rsqrt(spread + 1e-05)
    cells = cells * inv_std
    normed[...] = cells
    normed_bf[0:288] = cells.astype(BF)
    normed_bf[288:384] = jnp.zeros((96, 1024), BF)
    inv[...] = jnp.broadcast_to(inv_std, (288, 128))
    normed_t[...] = jnp.transpose(normed_bf[...], (1, 0)).reshape(32, 2, 16, 384)
    swaps = [send(normed_t.at[:, 1 - core], both_x.at[:, :, 384:768], t_send.at[1], t_recv.at[1], sibling)]
    grads[0:288] = gather(1).astype(BF)
    grads[288:384] = jnp.zeros((96, 1024), BF)
    grads_t[...] = jnp.transpose(grads[...], (1, 0)).reshape(32, 2, 16, 384)
    swaps.append(send(grads_t.at[:, 1 - core], both_g.at[:, :, 384:768], t_send.at[2], t_recv.at[2], sibling))
    both_x[:, :, 0:384] = normed_t[:, core]
    both_g[:, :, 0:384] = grads_t[:, core]

    for copy in own_weights:
        copy.wait()

    lane = lax.broadcasted_iota(jnp.int32, (WT, 128), 1)
    lower = lane < HD

    def split(value):
        zero = jnp.zeros_like(value)
        return jnp.concatenate([jnp.where(lower, value, zero), jnp.where(lower, zero, value)], axis=0)

    def weight(half, c):
        if half == 0:
            return (wq_ref[c] if c < 3 else wp_ref[...]).reshape(1024, 512)
        return other_ref[c].reshape(1024, 512)

    def project(half):
        for c in range(4):
            left = normed_bf if c < 3 else grads
            value = jnp.dot(left[0:288], weight(half, c), preferred_element_type=F32)
            value = value.astype(BF)
            if c == 0:
                value = value * jnp.asarray(0.125, BF)
            parts[c] = value

    def attend(half, start, stop):
        def pair(p, carry):
            span = pl.ds(pl.multiple_of(p * 128, 128), 128)
            for w in range(2):
                rows = pl.ds(w * WT, WT)
                q, k, v, g = (parts[c, rows, span] for c in range(4))
                qq, gg = split(q), split(g)
                bias = jnp.concatenate([bias_ref[half * 8 + 2 * p], bias_ref[half * 8 + 2 * p + 1]], axis=0)
                contract = (((1,), (1,)), ((), ()))
                flip = (((0,), (0,)), ((), ()))
                scores = lax.dot_general(qq, k, contract, preferred_element_type=F32) + bias
                weights = jnp.exp(scores)
                probs = weights / jnp.sum(weights, axis=1, keepdims=True)
                probs_bf = probs.astype(BF)
                found = jnp.dot(probs_bf, v, preferred_element_type=F32)
                dparts[half, 3, rows, span] = jnp.where(lower, found[0:WT], found[WT:]).astype(BF)
                gprobs = lax.dot_general(gg, v, contract, preferred_element_type=F32)
                dot_sum = jnp.sum(probs * gprobs, axis=1, keepdims=True)
                gscores = (probs * (gprobs - dot_sum)).astype(BF)
                gq = jnp.dot(gscores, k, preferred_element_type=F32)
                dparts[half, 0, rows, span] = (jnp.where(lower, gq[0:WT], gq[WT:]) * 0.125).astype(BF)
                dparts[half, 1, rows, span] = lax.dot_general(gscores, qq, flip, preferred_element_type=F32).astype(BF)
                dparts[half, 2, rows, span] = lax.dot_general(probs_bf, gg, flip, preferred_element_type=F32).astype(BF)
            return carry

        lax.fori_loop(start, stop, pair, 0)

    def input_grad(half):
        for c in range(3):
            value = lax.dot_general(dparts[half, c, 0:288], weight(half, c), (((1,), (1,)), ((), ())), preferred_element_type=F32)
            if half == 0 and c == 0:
                dx[...] = value
            else:
                dx[...] += value

    def swap(group, half, start, width):
        span = pl.ds(start, width)
        return send(dparts.at[half, :, 0:288, span], dparts.at[half, :, 384:672, span],
                    r_send.at[group, 0], r_recv.at[group, 0], sibling)

    def weight_grad(group, half, start, width, copy):
        mine, first_x, first_y = groups[group][0:3]
        span = pl.ds(start, width)
        copy.wait()
        stage = []
        for c in range(4):
            left = both_x if c < 3 else both_g
            value = jnp.dot(left[...].reshape(512, 768), dparts[half, c, :, span], preferred_element_type=F32)
            mine[c] = value.astype(BF).reshape(4, 2, 4, 16, width)
            for d in range(3):
                n = 1 + 3 * c + d
                if c % 2 == 0:
                    stage.append(send(mine.at[c, (x + d + 1) % 4], first_x.at[c // 2, d],
                                      r_send.at[group, n], r_recv.at[group, n], along_x[d]))
                else:
                    stage.append(send(mine.at[c, :, :, (y + d + 1) % 4], first_y.at[c // 2, d],
                                      r_send.at[group, n], r_recv.at[group, n], along_y[d]))
        return stage

    def plus(value, others):
        value = value.astype(F32)
        for d in range(3):
            value += others[d].astype(F32)
        return value

    def reduce_second(group, copies):
        mine, first_x, first_y, mid_x, mid_y, second_x, second_y = groups[group][0:7]
        for copy in copies:
            copy.wait()
        for n in range(2):
            mid_x[n] = plus(mine[2 * n, x], first_x[n]).astype(BF)
            mid_y[n] = plus(mine[2 * n + 1, :, :, y], first_y[n]).astype(BF)
        stage = []
        for d in range(3):
            stage.append(send(mid_x.at[:, :, (y + d + 1) % 4], second_x.at[d],
                              r_send.at[group, 13 + d], r_recv.at[group, 13 + d], along_y[d]))
            stage.append(send(mid_y.at[:, (x + d + 1) % 4], second_y.at[d],
                              r_send.at[group, 16 + d], r_recv.at[group, 16 + d], along_x[d]))
        return stage

    def reduce_third(group, copies):
        mid_x, mid_y, second_x, second_y, z_out, z_in = groups[group][3:9]
        for copy in copies:
            copy.wait()
        for n in range(2):
            z_out[2 * n] = plus(mid_x[n, :, y], [second_x[d, n] for d in range(3)]).astype(BF)
            z_out[2 * n + 1] = plus(mid_y[n, x], [second_y[d, n] for d in range(3)]).astype(BF)
        return [
            send(z_out.at[:, zl], z_in.at[0], r_send.at[group, 19], r_recv.at[group, 19], partner),
            send(z_out.at[:, 1 - zl], z_in.at[1], r_send.at[group, 20], r_recv.at[group, 20], diagonal),
        ]

    def early_grad(group, half, start, width, copy):
        mine, first_x, first_y, first_z = groups[group][0:4]
        span = pl.ds(start, width)
        copy.wait()
        stage = []
        for c in (2, 3, 0, 1):
            left = both_x if c < 3 else both_g
            value = jnp.dot(left[...].reshape(512, 768), dparts[half, c, :, span], preferred_element_type=F32)
            mine[c] = value.astype(BF).reshape(4, 2, 4, 16, width)
            if c == 3:
                stage.append(send(mine.at[2:4, :, 1 - zl], first_z, r_send.at[group, 1], r_recv.at[group, 1], along_z))
            for d in range(3):
                if c == 0:
                    stage.append(send(mine.at[0, (x + d + 1) % 4], first_x.at[d],
                                      r_send.at[group, 2 + d], r_recv.at[group, 2 + d], along_x[d]))
                if c == 1:
                    stage.append(send(mine.at[1, :, :, (y + d + 1) % 4], first_y.at[d],
                                      r_send.at[group, 5 + d], r_recv.at[group, 5 + d], along_y[d]))
        return stage

    def early_second(group, copies):
        mine, first_x, first_y, first_z, mid_x, mid_y, mid_z, second_x, second_y, second_zx, second_zy = groups[group][0:11]
        for copy in copies:
            copy.wait()
        mid_x[...] = plus(mine[0, x], first_x).astype(BF)
        mid_y[...] = plus(mine[1, :, :, y], first_y).astype(BF)
        mid_z[...] = (mine[2:4, :, zl].astype(F32) + first_z[...].astype(F32)).astype(BF)
        stage = []
        for d in range(3):
            to_x, to_y = (x + d + 1) % 4, (y + d + 1) % 4
            for n, (src, dst, target) in enumerate((
                (mid_z.at[0, to_x], second_zx.at[d], along_x[d]),
                (mid_z.at[1, :, to_y], second_zy.at[d], along_y[d]),
                (mid_x.at[:, to_y], second_x.at[d], along_y[d]),
                (mid_y.at[to_x], second_y.at[d], along_x[d]),
            )):
                stage.append(send(src, dst, r_send.at[group, 8 + 4 * d + n], r_recv.at[group, 8 + 4 * d + n], target))
        return stage

    def early_third(group, copies):
        (mid_x, mid_y, mid_z, second_x, second_y, second_zx, second_zy, z_out, z_in,
         late_x, late_y, third_x, third_y) = groups[group][4:17]
        for copy in copies:
            copy.wait()
        z_out[0] = plus(mid_x[:, y], second_x).astype(BF)
        z_out[1] = plus(mid_y[x], second_y).astype(BF)
        late_x[...] = plus(mid_z[0, x], second_zx).astype(BF)
        late_y[...] = plus(mid_z[1, :, y], second_zy).astype(BF)
        stage = [send(z_out.at[:, 1 - zl], z_in, r_send.at[group, 20], r_recv.at[group, 20], along_z)]
        for d in range(3):
            stage.append(send(late_x.at[(y + d + 1) % 4], third_x.at[d],
                              r_send.at[group, 21 + d], r_recv.at[group, 21 + d], along_y[d]))
            stage.append(send(late_y.at[(x + d + 1) % 4], third_y.at[d],
                              r_send.at[group, 24 + d], r_recv.at[group, 24 + d], along_x[d]))
        return stage

    def early_last(group, copies):
        z_out, z_in, late_x, late_y, third_x, third_y, done = groups[group][11:18]
        for copy in copies:
            copy.wait()
        for c in range(2):
            done[c] = z_out[c, zl].astype(F32) + z_in[c].astype(F32)
        done[2] = plus(late_x[y], third_x)
        done[3] = plus(late_y[x], third_y)

    project(0)
    attend(0, 0, 2)
    for copy in fourth:
        copy.wait()
    relay = []
    for d in (0, 2):
        from_y, from_x = (y + 3 - d) % 4, (x + 3 - d) % 4
        part = pl.ds(d, 2)
        share(other_ref.at[0:2, from_x, part, core], relay, 23 + d, along_x[d])
        share(other_ref.at[2:4, part, from_y, core], relay, 24 + d, along_y[d])
        share(other_ref.at[0:2, from_x, :, core], fifth, 17 + d, sibling)
        share(other_ref.at[2:4, :, from_y, core], fifth, 20 + d, sibling)
    attend(0, 2, 4)
    step = swap(0, 0, 0, 512)
    input_grad(0)
    for copy in swaps + relay:
        copy.wait()
    share(other_ref.at[0:2, (x + 2) % 4, :, core], fifth, 18, sibling)
    share(other_ref.at[2:4, :, (y + 2) % 4, core], fifth, 21, sibling)
    stage0 = early_grad(0, 0, 0, 512, step)
    for copy in fifth:
        copy.wait()
    project(1)
    attend(1, 0, 3)
    step = swap(1, 1, 0, 384)
    stage1 = weight_grad(1, 1, 0, 384, step)
    attend(1, 3, 4)
    step = swap(2, 1, 384, 128)
    input_grad(1)
    stage2 = weight_grad(2, 1, 384, 128, step)
    stage0 = early_second(0, stage0)

    total = dx[...]
    mean_grad = jnp.mean(total, axis=1, keepdims=True)
    mean_cross = jnp.mean(total * normed[...], axis=1, keepdims=True)
    result = (inv[:, 0:1] * (total - mean_grad - normed[...] * mean_cross)).astype(BF)
    moved = jnp.dot(placet_ref[...], result, preferred_element_type=F32).astype(BF)
    for di in range(2):
        for t in range(2):
            back[t, di] = moved[di * PIECE:(di + 1) * PIECE, t * 512:(t + 1) * 512]

    spans = (pl.ds(0, BIG), pl.ds(BIG, SMALL))
    pieces = []
    for n, (di, dj, to_tp, target) in enumerate(behind):
        pieces.append(send(back.at[to_tp, di, spans[dj]], landed.at[tp, di, spans[dj]],
                           back_send.at[n], back_recv.at[n], target))
    own = pltpu.make_async_copy(back.at[tp, 0, spans[0]], landed.at[tp, 0, spans[0]], local_sem.at[3])
    own.start()
    pieces.append(own)
    stage1 = reduce_second(1, stage1)
    stage0 = early_third(0, stage0)
    stage2 = reduce_second(2, stage2)
    stage1 = reduce_third(1, stage1)
    early_last(0, stage0)
    stage2 = reduce_third(2, stage2)
    for copy in pieces + stage1 + stage2:
        copy.wait()
    done = groups[0][17]
    for group, span in ((1, pl.ds(0, 384)), (2, pl.ds(384, 128))):
        others = groups[group][8]
        total_ref[:, :, span] = (done[:, :, span] + others[0].astype(F32) + others[1].astype(F32))


def early_scratch(width):
    shapes = ((4, 4, 2, 4), (3, 2, 4), (3, 4, 2), (2, 4, 4), (2, 4), (4, 2), (2, 4, 4),
              (3, 2), (3, 2), (3, 4), (3, 4), (2, 2), (2,), (4,), (4,), (3,), (3,))
    return [pltpu.VMEM(shape + (16, width), BF) for shape in shapes] + [pltpu.VMEM((4, 16, width), F32)]


def group_scratch(width):
    shapes = ((4, 4, 2, 4), (2, 3, 2, 4), (2, 3, 4, 2), (2, 2, 4), (2, 4, 2), (3, 2, 2), (3, 2, 2), (4, 2), (2, 4))
    return [pltpu.VMEM(shape + (16, width), BF) for shape in shapes]


def finish_kernel(landed, total_ref, packt_ref, tokens_ref, qkv_ref, proj_ref):
    for t in range(2):
        cells = landed[t].reshape(2 * PIECE, 512)
        moved = jnp.dot(packt_ref[...], cells, preferred_element_type=F32).astype(BF)
        if t == 0:
            tokens_ref[144:432, :] = moved
        else:
            tokens_ref[432:576, :] = moved[0:144]
            tokens_ref[0:144, :] = moved[144:288]
    qkv_ref[...] = total_ref[0:3]
    proj_ref[...] = total_ref[3]


VM = pl.BlockSpec(memory_space=pltpu.VMEM)
HB = pl.BlockSpec(memory_space=pl.ANY)
LIMIT = 60 * 1024 * 1024


def shards(tokens, w_qkv, w_proj, bias_table, bias_index, regions, out_grad):
    flat_in = tokens.reshape(576, 512)
    flat_grad = out_grad.reshape(576, 512)
    wq = w_qkv.transpose(1, 0, 2).reshape(3, 32, 32, 512)
    wp = w_proj.reshape(32, 32, 512)
    pack = jnp.asarray(PACK, BF)
    packt = jnp.asarray(UNPACK, BF)
    place = jnp.asarray(PLACE, BF)
    placet = jnp.asarray(LEAVE, BF)
    dma = pltpu.SemaphoreType.DMA
    shape = jax.ShapeDtypeStruct
    vmem = pltpu.VMEM
    landed, total = pl.pallas_call(
        whole_kernel,
        out_shape=(shape((2, 2, PIECE, 512), BF), shape((4, 16, 512), F32)),
        in_specs=[VM] * 5 + [HB] * 2 + [VM] * 3,
        out_specs=(VM, VM),
        scratch_shapes=[
            vmem((3, 32, 32, 512), BF), vmem((32, 32, 512), BF),
            vmem((4, 4, 4, 2, 32, 512), BF), vmem((2, 8, 768), F32),
            vmem((2, 2, BOTH, 512), BF), vmem((2, 2, BOTH, 512), BF), vmem((16, WT, WT), F32),
            vmem((288, 1024), F32), vmem((384, 1024), BF), vmem((384, 1024), BF),
            vmem((32, 2, 16, 384), BF), vmem((32, 2, 16, 384), BF), vmem((32, 16, 768), BF), vmem((32, 16, 768), BF),
            vmem((288, 128), F32), vmem((4, 288, 512), BF), vmem((2, 4, 768, 512), BF),
            vmem((288, 1024), F32), vmem((2, 2, PIECE, 512), BF),
            *early_scratch(512), *group_scratch(384), *group_scratch(128),
            dma((7,)), dma((7,)), dma((7,)), dma((7,)), dma((27,)), dma((27,)), dma((3, 27)), dma((3, 27)), dma((3,)), dma((3,)), dma((4,)),
        ],
        compiler_params=pltpu.CompilerParams(collective_id=0, has_side_effects=True, vmem_limit_bytes=LIMIT),
        name="whole",
    )(flat_in, flat_grad, pack, place, placet, wq, wp, bias_table.T, bias_index, regions.transpose(1, 0, 2))

    grad_tokens, qkv_grad, proj_grad = pl.pallas_call(
        finish_kernel,
        out_shape=(shape((576, 512), BF), shape((3, 16, 512), F32), shape((16, 512), F32)),
        in_specs=[VM] * 3,
        out_specs=(VM, VM, VM),
        name="finish",
    )(landed, total, packt)
    return grad_tokens.reshape(tokens.shape), qkv_grad.transpose(1, 0, 2), proj_grad


def solution(mesh):
    in_specs = (
        P(None, "lat", "lon", "tp"),
        P(None, None, "tp"),
        P(None, "tp"),
        P(None, "tp"),
        P(),
        P(None, "lat", "lon"),
        P(None, "lat", "lon", "tp"),
    )
    out_specs = (
        P(None, "lat", "lon", "tp"),
        P(("lat", "lon"), None, "tp"),
        P(("lat", "lon"), "tp"),
    )
    return jax.shard_map(shards, mesh=mesh, in_specs=in_specs, out_specs=out_specs, check_vma=False)
```

```python
import functools

import jax
import jax.numpy as jnp
import numpy as np
from jax import lax
from jax.experimental import pallas as pl
from jax.experimental.pallas import tpu as pltpu
from jax.sharding import PartitionSpec as P

HD = 64
WT = 144
BIG = 112
SMALL = 48
PIECE = BIG + SMALL
BOTH_BIG = 224
BOTH_SMALL = 80
BOTH = BOTH_BIG + BOTH_SMALL
MESH = pl.DeviceIdType.MESH
BF = jnp.bfloat16
F32 = jnp.float32
FAR = -1e30


def permutations():
    pack = np.zeros((2, BOTH, 576), np.float32)
    place = np.zeros((2, 288, 2 * BOTH), np.float32)
    leave = np.zeros((2 * PIECE, 288), np.float32)
    unpack = np.zeros((288, 2 * PIECE), np.float32)
    for di in range(2):
        for lv in range(2):
            for row in range(3):
                local = row + (3 if di == 0 else 0)
                for col in range(24):
                    cell = lv * 144 + local * 24 + col
                    shifted = (col - 6) % 24
                    window = (shifted // 12) * 144 + lv * 72 + (row + 3 * di) * 12 + shifted % 12
                    big = lv * 54 + row * 18 + col - 6
                    small = lv * 18 + row * 6 + col
                    for which in range(2):
                        spot = which * 108 + big if col >= 6 else BOTH_BIG + which * 36 + small
                        pack[di, spot, which * 288 + cell] = 1
                        place[which, window, di * BOTH + spot] = 1
                    spot = big if col >= 6 else BIG + small
                    leave[di * PIECE + spot, window] = 1
                    unpack[cell, di * PIECE + spot] = 1
    return pack, place, leave, unpack


PACK, PLACE, LEAVE, UNPACK = permutations()


def position():
    lat, lon, tp = lax.axis_index("lat"), lax.axis_index("lon"), lax.axis_index("tp")
    return lat, lon, tp


def device(lat, lon, tp):
    return {"lat": lat, "lon": lon, "tp": tp}


def neighbours():
    lat, lon, tp = position()
    x, zl, y, core = lat // 2, lat % 2, lon // 2, lon % 2
    sibling = device(lat, y * 2 + 1 - core, tp)
    along_x = [device(((x + d) % 4) * 2 + zl, lon, tp) for d in (1, 2, 3)]
    along_y = [device(lat, ((y + d) % 4) * 2 + core, tp) for d in (1, 2, 3)]
    along_z = device(x * 2 + 1 - zl, lon, tp)
    partner = device(lat, lon, 1 - tp)
    return x, zl, y, core, sibling, along_x, along_y, along_z, partner


def piece_ends(sign):
    lat, lon, tp = position()
    ends = []
    for di in range(2):
        for dj in range(2):
            for other in range(2):
                if di == 0 and dj == 0 and other == 0:
                    continue
                to_tp = 1 - tp if other else tp
                ends.append((di, dj, to_tp, device((lat + sign * di + 8) % 8, (lon + sign * dj + 8) % 8, to_tp)))
    return ends


def send(src, dst, send_sem, recv_sem, target):
    copy = pltpu.make_async_remote_copy(
        src_ref=src, dst_ref=dst, send_sem=send_sem, recv_sem=recv_sem, device_id=target, device_id_type=MESH
    )
    copy.start()
    return copy


def whole_kernel(tok_ref, grad_ref, pack_ref, place_ref, placet_ref, wq_hbm, wp_hbm, table_ref, index_ref, regions_ref,
                 landed, total_ref,
                 wq_ref, wp_ref, other_ref, tables_ref, packed, held, bias_ref,
                 normed, normed_bf, grads, normed_t, grads_t, both_x, both_g, inv, parts, dparts, dx, back,
                 *rest):
    groups, sems = (rest[0:18], rest[18:27], rest[27:36]), rest[36:]
    (piece_send, piece_recv, back_send, back_recv, w_send, w_recv, r_send, r_recv, t_send, t_recv, local_sem) = sems
    lat, lon, tp = position()
    x, zl, y, core, sibling, along_x, along_y, along_z, partner = neighbours()
    ahead, behind = piece_ends(-1), piece_ends(1)
    barrier = pltpu.get_barrier_semaphore()
    diagonal = device(x * 2 + 1 - zl, lon, 1 - tp)
    targets = [diagonal] + [e[3] for e in ahead] + [e[3] for e in behind] + [sibling, along_z, partner] + along_x + along_y
    for target in targets:
        pl.semaphore_signal(barrier, inc=1, device_id=target, device_id_type=MESH)

    own_weights = [
        pltpu.make_async_copy(wq_hbm, wq_ref, local_sem.at[0]),
        pltpu.make_async_copy(wp_hbm, wp_ref, local_sem.at[1]),
    ]
    for copy in own_weights:
        copy.start()

    tables_ref[0] = jnp.zeros((8, 768), F32)
    tables_ref[0, :, 0:759] = table_ref[...]

    def pack(half):
        cells = []
        for ref in (tok_ref, grad_ref):
            if half == 0:
                cells.append(ref[144:432, :])
            else:
                cells.extend([ref[432:576, :], ref[0:144, :]])
        cells = jnp.concatenate(cells, axis=0)
        for di in range(2):
            packed[half, di] = jnp.dot(pack_ref[di], cells, preferred_element_type=F32).astype(BF)

    pl.semaphore_wait(barrier, len(targets))

    mine = (x * 4 + y) * 2 + core
    first = [
        send(wq_hbm.at[:, mine], other_ref.at[0:3, x, y, core], w_send.at[0], w_recv.at[0], partner),
        send(wp_hbm.at[mine], other_ref.at[3, x, y, core], w_send.at[1], w_recv.at[1], partner),
        send(tables_ref.at[0], tables_ref.at[1], w_send.at[2], w_recv.at[2], partner),
    ]
    spans = (pl.ds(0, BOTH_BIG), pl.ds(BOTH_BIG, BOTH_SMALL))
    pack(0)
    pack(1)
    pieces = []
    for n, (di, dj, to_tp, target) in enumerate(ahead):
        pieces.append(send(packed.at[to_tp, di, spans[dj]], held.at[tp, di, spans[dj]],
                           piece_send.at[n], piece_recv.at[n], target))
    own = pltpu.make_async_copy(packed.at[tp, 0, spans[0]], held.at[tp, 0, spans[0]], local_sem.at[2])
    own.start()
    pieces.append(own)

    for half in range(2):
        for c in range(4):
            for base in (288, 672):
                dparts[half, c, base:base + 96] = jnp.zeros((96, 512), BF)

    rows = lax.broadcasted_iota(jnp.int32, (WT, WT), 0) // 12
    cols = lax.broadcasted_iota(jnp.int32, (WT, WT), 1) // 12
    left = jnp.zeros((WT, WT), jnp.int32)
    right = jnp.zeros((WT, WT), jnp.int32)
    for lv in range(2):
        for row in range(6):
            value = regions_ref[row, pl.ds(2 * tp + lv, 1), 0:1]
            left = jnp.where(rows == lv * 6 + row, value, left)
            right = jnp.where(cols == lv * 6 + row, value, right)
    blocked = jnp.where(left == right, 0.0, FAR).astype(F32)

    first.pop().wait()
    blocks = []
    for s in range(2):
        table = tables_ref[s]
        top = table.astype(BF).astype(F32)
        rest = table - top
        mid = rest.astype(BF).astype(F32)
        low = rest - mid
        for part in (top, mid, low):
            for g in range(3):
                blocks.append(part[:, g * 256:(g + 1) * 256])
    matrix = jnp.concatenate(blocks, axis=0).astype(BF)
    depth = lax.broadcasted_iota(jnp.int32, (256, WT), 0)

    def some_rows(step, carry):
        found = ([], [])
        index = index_ref[pl.ds(pl.multiple_of(step * 8, 8), 8), :]
        for r in range(8):
            row = index[r:r + 1, :]
            low_part, high_part = row & 255, row >> 8
            hot = jnp.where(depth == low_part, 1.0, 0.0).astype(BF)
            picked = jnp.dot(matrix, hot, preferred_element_type=F32)
            for s in range(2):
                total = jnp.zeros((8, WT), F32)
                for g in range(3):
                    base = s * 72 + g * 8
                    value = picked[base:base + 8] + picked[base + 24:base + 32] + picked[base + 48:base + 56]
                    total = jnp.where(high_part == g, value, total)
                found[s].append(total)
        for s in range(2):
            stacked = jnp.stack(found[s], axis=0)
            bias_ref[s * 8:(s + 1) * 8, pl.ds(pl.multiple_of(step * 8, 8), 8), :] = jnp.transpose(stacked, (1, 0, 2))
        return carry

    lax.fori_loop(0, 4, some_rows, 0)
    for copy in first:
        copy.wait()

    def share(part, copies, n, target):
        copies.append(send(part, part, w_send.at[n], w_recv.at[n], target))

    third, fourth, fifth = [], [], []
    for d in range(3):
        share(other_ref.at[0:2, x, y, core], third, 3 + d, along_y[d])
        share(other_ref.at[2:4, x, y, core], third, 6 + d, along_x[d])
    lax.fori_loop(4, 10, some_rows, 0)
    lax.fori_loop(10, WT // 8, some_rows, 0)
    for h in range(16):
        bias_ref[h] = bias_ref[h] + blocked

    for copy in third + pieces:
        copy.wait()
    for d in (0, 2):
        share(other_ref.at[0:2, x, :, core], fourth, 9 + d, along_x[d])
        share(other_ref.at[2:4, :, y, core], fourth, 12 + d, along_y[d])
    share(other_ref.at[0:2, x, :, core], fifth, 15, sibling)
    share(other_ref.at[2:4, :, y, core], fifth, 16, sibling)

    def gather(which):
        halves = []
        for t in range(2):
            rows = held[t].reshape(2 * BOTH, 512)
            halves.append(jnp.dot(place_ref[which], rows, preferred_element_type=F32))
        return jnp.concatenate(halves, axis=1)

    cells = gather(0)
    center = jnp.mean(cells, axis=1, keepdims=True)
    cells = cells - center
    spread = jnp.mean(jnp.square(cells), axis=1, keepdims=True)
    inv_std = lax.rsqrt(spread + 1e-05)
    cells = cells * inv_std
    normed[...] = cells
    normed_bf[0:288] = cells.astype(BF)
    normed_bf[288:384] = jnp.zeros((96, 1024), BF)
    inv[...] = jnp.broadcast_to(inv_std, (288, 128))
    normed_t[...] = jnp.transpose(normed_bf[...], (1, 0)).reshape(32, 2, 16, 384)
    swaps = [send(normed_t.at[:, 1 - core], both_x.at[:, :, 384:768], t_send.at[1], t_recv.at[1], sibling)]
    grads[0:288] = gather(1).astype(BF)
    grads[288:384] = jnp.zeros((96, 1024), BF)
    grads_t[...] = jnp.transpose(grads[...], (1, 0)).reshape(32, 2, 16, 384)
    swaps.append(send(grads_t.at[:, 1 - core], both_g.at[:, :, 384:768], t_send.at[2], t_recv.at[2], sibling))
    both_x[:, :, 0:384] = normed_t[:, core]
    both_g[:, :, 0:384] = grads_t[:, core]

    for copy in own_weights:
        copy.wait()

    lane = lax.broadcasted_iota(jnp.int32, (WT, 128), 1)
    lower = lane < HD

    def split(value):
        zero = jnp.zeros_like(value)
        return jnp.concatenate([jnp.where(lower, value, zero), jnp.where(lower, zero, value)], axis=0)

    def weight(half, c):
        if half == 0:
            return (wq_ref[c] if c < 3 else wp_ref[...]).reshape(1024, 512)
        return other_ref[c].reshape(1024, 512)

    def project(half):
        for c in range(4):
            left = normed_bf if c < 3 else grads
            value = jnp.dot(left[0:288], weight(half, c), preferred_element_type=F32)
            value = value.astype(BF)
            if c == 0:
                value = value * jnp.asarray(0.125, BF)
            parts[c] = value

    def attend(half, start, stop):
        def pair(p, carry):
            span = pl.ds(pl.multiple_of(p * 128, 128), 128)
            for w in range(2):
                rows = pl.ds(w * WT, WT)
                q, k, v, g = (parts[c, rows, span] for c in range(4))
                qq, gg = split(q), split(g)
                bias = jnp.concatenate([bias_ref[half * 8 + 2 * p], bias_ref[half * 8 + 2 * p + 1]], axis=0)
                contract = (((1,), (1,)), ((), ()))
                flip = (((0,), (0,)), ((), ()))
                scores = lax.dot_general(qq, k, contract, preferred_element_type=F32) + bias
                weights = jnp.exp(scores)
                probs = weights / jnp.sum(weights, axis=1, keepdims=True)
                probs_bf = probs.astype(BF)
                found = jnp.dot(probs_bf, v, preferred_element_type=F32)
                dparts[half, 3, rows, span] = jnp.where(lower, found[0:WT], found[WT:]).astype(BF)
                gprobs = lax.dot_general(gg, v, contract, preferred_element_type=F32)
                dot_sum = jnp.sum(probs * gprobs, axis=1, keepdims=True)
                gscores = (probs * (gprobs - dot_sum)).astype(BF)
                gq = jnp.dot(gscores, k, preferred_element_type=F32)
                dparts[half, 0, rows, span] = (jnp.where(lower, gq[0:WT], gq[WT:]) * 0.125).astype(BF)
                dparts[half, 1, rows, span] = lax.dot_general(gscores, qq, flip, preferred_element_type=F32).astype(BF)
                dparts[half, 2, rows, span] = lax.dot_general(probs_bf, gg, flip, preferred_element_type=F32).astype(BF)
            return carry

        lax.fori_loop(start, stop, pair, 0)

    def input_grad(half):
        for c in range(3):
            value = lax.dot_general(dparts[half, c, 0:288], weight(half, c), (((1,), (1,)), ((), ())), preferred_element_type=F32)
            if half == 0 and c == 0:
                dx[...] = value
            else:
                dx[...] += value

    def swap(group, half, start, width):
        span = pl.ds(start, width)
        return send(dparts.at[half, :, 0:288, span], dparts.at[half, :, 384:672, span],
                    r_send.at[group, 0], r_recv.at[group, 0], sibling)

    def weight_grad(group, half, start, width, copy):
        mine, first_x, first_y = groups[group][0:3]
        span = pl.ds(start, width)
        copy.wait()
        stage = []
        for c in range(4):
            left = both_x if c < 3 else both_g
            value = jnp.dot(left[...].reshape(512, 768), dparts[half, c, :, span], preferred_element_type=F32)
            mine[c] = value.astype(BF).reshape(4, 2, 4, 16, width)
            for d in range(3):
                n = 1 + 3 * c + d
                if c % 2 == 0:
                    stage.append(send(mine.at[c, (x + d + 1) % 4], first_x.at[c // 2, d],
                                      r_send.at[group, n], r_recv.at[group, n], along_x[d]))
                else:
                    stage.append(send(mine.at[c, :, :, (y + d + 1) % 4], first_y.at[c // 2, d],
                                      r_send.at[group, n], r_recv.at[group, n], along_y[d]))
        return stage

    def plus(value, others):
        value = value.astype(F32)
        for d in range(3):
            value += others[d].astype(F32)
        return value

    def reduce_second(group, copies):
        mine, first_x, first_y, mid_x, mid_y, second_x, second_y = groups[group][0:7]
        for copy in copies:
            copy.wait()
        for n in range(2):
            mid_x[n] = plus(mine[2 * n, x], first_x[n]).astype(BF)
            mid_y[n] = plus(mine[2 * n + 1, :, :, y], first_y[n]).astype(BF)
        stage = []
        for d in range(3):
            stage.append(send(mid_x.at[:, :, (y + d + 1) % 4], second_x.at[d],
                              r_send.at[group, 13 + d], r_recv.at[group, 13 + d], along_y[d]))
            stage.append(send(mid_y.at[:, (x + d + 1) % 4], second_y.at[d],
                              r_send.at[group, 16 + d], r_recv.at[group, 16 + d], along_x[d]))
        return stage

    def reduce_third(group, copies):
        mid_x, mid_y, second_x, second_y, z_out, z_in = groups[group][3:9]
        for copy in copies:
            copy.wait()
        for n in range(2):
            z_out[2 * n] = plus(mid_x[n, :, y], [second_x[d, n] for d in range(3)]).astype(BF)
            z_out[2 * n + 1] = plus(mid_y[n, x], [second_y[d, n] for d in range(3)]).astype(BF)
        return [
            send(z_out.at[:, zl], z_in.at[0], r_send.at[group, 19], r_recv.at[group, 19], partner),
            send(z_out.at[:, 1 - zl], z_in.at[1], r_send.at[group, 20], r_recv.at[group, 20], diagonal),
        ]

    def early_grad(group, half, start, width, copy):
        mine, first_x, first_y, first_z = groups[group][0:4]
        span = pl.ds(start, width)
        copy.wait()
        stage = []
        for c in (2, 3, 0, 1):
            left = both_x if c < 3 else both_g
            value = jnp.dot(left[...].reshape(512, 768), dparts[half, c, :, span], preferred_element_type=F32)
            mine[c] = value.astype(BF).reshape(4, 2, 4, 16, width)
            if c == 3:
                stage.append(send(mine.at[2:4, :, 1 - zl], first_z, r_send.at[group, 1], r_recv.at[group, 1], along_z))
            for d in range(3):
                if c == 0:
                    stage.append(send(mine.at[0, (x + d + 1) % 4], first_x.at[d],
                                      r_send.at[group, 2 + d], r_recv.at[group, 2 + d], along_x[d]))
                if c == 1:
                    stage.append(send(mine.at[1, :, :, (y + d + 1) % 4], first_y.at[d],
                                      r_send.at[group, 5 + d], r_recv.at[group, 5 + d], along_y[d]))
        return stage

    def early_second(group, copies):
        mine, first_x, first_y, first_z, mid_x, mid_y, mid_z, second_x, second_y, second_zx, second_zy = groups[group][0:11]
        for copy in copies:
            copy.wait()
        mid_x[...] = plus(mine[0, x], first_x).astype(BF)
        mid_y[...] = plus(mine[1, :, :, y], first_y).astype(BF)
        mid_z[...] = (mine[2:4, :, zl].astype(F32) + first_z[...].astype(F32)).astype(BF)
        stage = []
        for d in range(3):
            to_x, to_y = (x + d + 1) % 4, (y + d + 1) % 4
            for n, (src, dst, target) in enumerate((
                (mid_z.at[0, to_x], second_zx.at[d], along_x[d]),
                (mid_z.at[1, :, to_y], second_zy.at[d], along_y[d]),
                (mid_x.at[:, to_y], second_x.at[d], along_y[d]),
                (mid_y.at[to_x], second_y.at[d], along_x[d]),
            )):
                stage.append(send(src, dst, r_send.at[group, 8 + 4 * d + n], r_recv.at[group, 8 + 4 * d + n], target))
        return stage

    def early_third(group, copies):
        (mid_x, mid_y, mid_z, second_x, second_y, second_zx, second_zy, z_out, z_in,
         late_x, late_y, third_x, third_y) = groups[group][4:17]
        for copy in copies:
            copy.wait()
        z_out[0] = plus(mid_x[:, y], second_x).astype(BF)
        z_out[1] = plus(mid_y[x], second_y).astype(BF)
        late_x[...] = plus(mid_z[0, x], second_zx).astype(BF)
        late_y[...] = plus(mid_z[1, :, y], second_zy).astype(BF)
        stage = [send(z_out.at[:, 1 - zl], z_in, r_send.at[group, 20], r_recv.at[group, 20], along_z)]
        for d in range(3):
            stage.append(send(late_x.at[(y + d + 1) % 4], third_x.at[d],
                              r_send.at[group, 21 + d], r_recv.at[group, 21 + d], along_y[d]))
            stage.append(send(late_y.at[(x + d + 1) % 4], third_y.at[d],
                              r_send.at[group, 24 + d], r_recv.at[group, 24 + d], along_x[d]))
        return stage

    def early_last(group, copies):
        z_out, z_in, late_x, late_y, third_x, third_y, done = groups[group][11:18]
        for copy in copies:
            copy.wait()
        for c in range(2):
            done[c] = z_out[c, zl].astype(F32) + z_in[c].astype(F32)
        done[2] = plus(late_x[y], third_x)
        done[3] = plus(late_y[x], third_y)

    project(0)
    attend(0, 0, 2)
    for copy in fourth:
        copy.wait()
    relay = []
    for d in (0, 2):
        from_y, from_x = (y + 3 - d) % 4, (x + 3 - d) % 4
        part = pl.ds(d, 2)
        share(other_ref.at[0:2, from_x, part, core], relay, 23 + d, along_x[d])
        share(other_ref.at[2:4, part, from_y, core], relay, 24 + d, along_y[d])
        share(other_ref.at[0:2, from_x, :, core], fifth, 17 + d, sibling)
        share(other_ref.at[2:4, :, from_y, core], fifth, 20 + d, sibling)
    attend(0, 2, 4)
    step = swap(0, 0, 0, 512)
    input_grad(0)
    for copy in swaps + relay:
        copy.wait()
    share(other_ref.at[0:2, (x + 2) % 4, :, core], fifth, 18, sibling)
    share(other_ref.at[2:4, :, (y + 2) % 4, core], fifth, 21, sibling)
    stage0 = early_grad(0, 0, 0, 512, step)
    for copy in fifth:
        copy.wait()
    project(1)
    attend(1, 0, 2)
    step = swap(1, 1, 0, 256)
    attend(1, 2, 3)
    stage1 = weight_grad(1, 1, 0, 256, step)
    attend(1, 3, 4)
    step = swap(2, 1, 256, 256)
    input_grad(1)
    stage2 = weight_grad(2, 1, 256, 256, step)
    stage0 = early_second(0, stage0)

    total = dx[...]
    mean_grad = jnp.mean(total, axis=1, keepdims=True)
    mean_cross = jnp.mean(total * normed[...], axis=1, keepdims=True)
    result = (inv[:, 0:1] * (total - mean_grad - normed[...] * mean_cross)).astype(BF)
    moved = jnp.dot(placet_ref[...], result, preferred_element_type=F32).astype(BF)
    for di in range(2):
        for t in range(2):
            back[t, di] = moved[di * PIECE:(di + 1) * PIECE, t * 512:(t + 1) * 512]

    spans = (pl.ds(0, BIG), pl.ds(BIG, SMALL))
    pieces = []
    for n, (di, dj, to_tp, target) in enumerate(behind):
        pieces.append(send(back.at[to_tp, di, spans[dj]], landed.at[tp, di, spans[dj]],
                           back_send.at[n], back_recv.at[n], target))
    own = pltpu.make_async_copy(back.at[tp, 0, spans[0]], landed.at[tp, 0, spans[0]], local_sem.at[3])
    own.start()
    pieces.append(own)
    stage1 = reduce_second(1, stage1)
    stage0 = early_third(0, stage0)
    stage2 = reduce_second(2, stage2)
    stage1 = reduce_third(1, stage1)
    early_last(0, stage0)
    stage2 = reduce_third(2, stage2)
    for copy in pieces + stage1 + stage2:
        copy.wait()
    done = groups[0][17]
    for group, span in ((1, pl.ds(0, 256)), (2, pl.ds(256, 256))):
        others = groups[group][8]
        total_ref[:, :, span] = (done[:, :, span] + others[0].astype(F32) + others[1].astype(F32))


def early_scratch(width):
    shapes = ((4, 4, 2, 4), (3, 2, 4), (3, 4, 2), (2, 4, 4), (2, 4), (4, 2), (2, 4, 4),
              (3, 2), (3, 2), (3, 4), (3, 4), (2, 2), (2,), (4,), (4,), (3,), (3,))
    return [pltpu.VMEM(shape + (16, width), BF) for shape in shapes] + [pltpu.VMEM((4, 16, width), F32)]


def group_scratch(width):
    shapes = ((4, 4, 2, 4), (2, 3, 2, 4), (2, 3, 4, 2), (2, 2, 4), (2, 4, 2), (3, 2, 2), (3, 2, 2), (4, 2), (2, 4))
    return [pltpu.VMEM(shape + (16, width), BF) for shape in shapes]


def finish_kernel(landed, total_ref, packt_ref, tokens_ref, qkv_ref, proj_ref):
    for t in range(2):
        cells = landed[t].reshape(2 * PIECE, 512)
        moved = jnp.dot(packt_ref[...], cells, preferred_element_type=F32).astype(BF)
        if t == 0:
            tokens_ref[144:432, :] = moved
        else:
            tokens_ref[432:576, :] = moved[0:144]
            tokens_ref[0:144, :] = moved[144:288]
    qkv_ref[...] = total_ref[0:3]
    proj_ref[...] = total_ref[3]


VM = pl.BlockSpec(memory_space=pltpu.VMEM)
HB = pl.BlockSpec(memory_space=pl.ANY)
LIMIT = 60 * 1024 * 1024


def shards(tokens, w_qkv, w_proj, bias_table, bias_index, regions, out_grad):
    flat_in = tokens.reshape(576, 512)
    flat_grad = out_grad.reshape(576, 512)
    wq = w_qkv.transpose(1, 0, 2).reshape(3, 32, 32, 512)
    wp = w_proj.reshape(32, 32, 512)
    pack = jnp.asarray(PACK, BF)
    packt = jnp.asarray(UNPACK, BF)
    place = jnp.asarray(PLACE, BF)
    placet = jnp.asarray(LEAVE, BF)
    dma = pltpu.SemaphoreType.DMA
    shape = jax.ShapeDtypeStruct
    vmem = pltpu.VMEM
    landed, total = pl.pallas_call(
        whole_kernel,
        out_shape=(shape((2, 2, PIECE, 512), BF), shape((4, 16, 512), F32)),
        in_specs=[VM] * 5 + [HB] * 2 + [VM] * 3,
        out_specs=(VM, VM),
        scratch_shapes=[
            vmem((3, 32, 32, 512), BF), vmem((32, 32, 512), BF),
            vmem((4, 4, 4, 2, 32, 512), BF), vmem((2, 8, 768), F32),
            vmem((2, 2, BOTH, 512), BF), vmem((2, 2, BOTH, 512), BF), vmem((16, WT, WT), F32),
            vmem((288, 1024), F32), vmem((384, 1024), BF), vmem((384, 1024), BF),
            vmem((32, 2, 16, 384), BF), vmem((32, 2, 16, 384), BF), vmem((32, 16, 768), BF), vmem((32, 16, 768), BF),
            vmem((288, 128), F32), vmem((4, 288, 512), BF), vmem((2, 4, 768, 512), BF),
            vmem((288, 1024), F32), vmem((2, 2, PIECE, 512), BF),
            *early_scratch(512), *group_scratch(256), *group_scratch(256),
            dma((7,)), dma((7,)), dma((7,)), dma((7,)), dma((27,)), dma((27,)), dma((3, 27)), dma((3, 27)), dma((3,)), dma((3,)), dma((4,)),
        ],
        compiler_params=pltpu.CompilerParams(collective_id=0, has_side_effects=True, vmem_limit_bytes=LIMIT),
        name="whole",
    )(flat_in, flat_grad, pack, place, placet, wq, wp, bias_table.T, bias_index, regions.transpose(1, 0, 2))

    grad_tokens, qkv_grad, proj_grad = pl.pallas_call(
        finish_kernel,
        out_shape=(shape((576, 512), BF), shape((3, 16, 512), F32), shape((16, 512), F32)),
        in_specs=[VM] * 3,
        out_specs=(VM, VM, VM),
        name="finish",
    )(landed, total, packt)
    return grad_tokens.reshape(tokens.shape), qkv_grad.transpose(1, 0, 2), proj_grad


def solution(mesh):
    in_specs = (
        P(None, "lat", "lon", "tp"),
        P(None, None, "tp"),
        P(None, "tp"),
        P(None, "tp"),
        P(),
        P(None, "lat", "lon"),
        P(None, "lat", "lon", "tp"),
    )
    out_specs = (
        P(None, "lat", "lon", "tp"),
        P(("lat", "lon"), None, "tp"),
        P(("lat", "lon"), "tp"),
    )
    return jax.shard_map(shards, mesh=mesh, in_specs=in_specs, out_specs=out_specs, check_vma=False)
```

```python
import functools

import jax
import jax.numpy as jnp
import numpy as np
from jax import lax
from jax.experimental import pallas as pl
from jax.experimental.pallas import tpu as pltpu
from jax.sharding import PartitionSpec as P

HD = 64
WT = 144
BIG = 112
SMALL = 48
PIECE = BIG + SMALL
BOTH_BIG = 224
BOTH_SMALL = 80
BOTH = BOTH_BIG + BOTH_SMALL
MESH = pl.DeviceIdType.MESH
BF = jnp.bfloat16
F32 = jnp.float32
FAR = -1e30


def permutations():
    pack = np.zeros((2, BOTH, 576), np.float32)
    place = np.zeros((2, 288, 2 * BOTH), np.float32)
    leave = np.zeros((2 * PIECE, 288), np.float32)
    unpack = np.zeros((288, 2 * PIECE), np.float32)
    for di in range(2):
        for lv in range(2):
            for row in range(3):
                local = row + (3 if di == 0 else 0)
                for col in range(24):
                    cell = lv * 144 + local * 24 + col
                    shifted = (col - 6) % 24
                    window = (shifted // 12) * 144 + lv * 72 + (row + 3 * di) * 12 + shifted % 12
                    big = lv * 54 + row * 18 + col - 6
                    small = lv * 18 + row * 6 + col
                    for which in range(2):
                        spot = which * 108 + big if col >= 6 else BOTH_BIG + which * 36 + small
                        pack[di, spot, which * 288 + cell] = 1
                        place[which, window, di * BOTH + spot] = 1
                    spot = big if col >= 6 else BIG + small
                    leave[di * PIECE + spot, window] = 1
                    unpack[cell, di * PIECE + spot] = 1
    return pack, place, leave, unpack


PACK, PLACE, LEAVE, UNPACK = permutations()


def position():
    lat, lon, tp = lax.axis_index("lat"), lax.axis_index("lon"), lax.axis_index("tp")
    return lat, lon, tp


def device(lat, lon, tp):
    return {"lat": lat, "lon": lon, "tp": tp}


def neighbours():
    lat, lon, tp = position()
    x, zl, y, core = lat // 2, lat % 2, lon // 2, lon % 2
    sibling = device(lat, y * 2 + 1 - core, tp)
    along_x = [device(((x + d) % 4) * 2 + zl, lon, tp) for d in (1, 2, 3)]
    along_y = [device(lat, ((y + d) % 4) * 2 + core, tp) for d in (1, 2, 3)]
    along_z = device(x * 2 + 1 - zl, lon, tp)
    partner = device(lat, lon, 1 - tp)
    return x, zl, y, core, sibling, along_x, along_y, along_z, partner


def piece_ends(sign):
    lat, lon, tp = position()
    ends = []
    for di in range(2):
        for dj in range(2):
            for other in range(2):
                if di == 0 and dj == 0 and other == 0:
                    continue
                to_tp = 1 - tp if other else tp
                ends.append((di, dj, to_tp, device((lat + sign * di + 8) % 8, (lon + sign * dj + 8) % 8, to_tp)))
    return ends


def send(src, dst, send_sem, recv_sem, target):
    copy = pltpu.make_async_remote_copy(
        src_ref=src, dst_ref=dst, send_sem=send_sem, recv_sem=recv_sem, device_id=target, device_id_type=MESH
    )
    copy.start()
    return copy


def whole_kernel(tok_ref, grad_ref, pack_ref, place_ref, placet_ref, wq_hbm, wp_hbm, table_ref, index_ref, regions_ref,
                 landed, total_ref,
                 wq_ref, wp_ref, other_ref, tables_ref, packed, held, bias_ref,
                 normed, normed_bf, grads, normed_t, grads_t, both_x, both_g, inv, parts, dparts, dx, back,
                 *rest):
    groups, sems = (rest[0:18], rest[18:27], rest[27:36]), rest[36:]
    (piece_send, piece_recv, back_send, back_recv, w_send, w_recv, r_send, r_recv, t_send, t_recv, local_sem) = sems
    lat, lon, tp = position()
    x, zl, y, core, sibling, along_x, along_y, along_z, partner = neighbours()
    ahead, behind = piece_ends(-1), piece_ends(1)
    barrier = pltpu.get_barrier_semaphore()
    diagonal = device(x * 2 + 1 - zl, lon, 1 - tp)
    targets = [diagonal] + [e[3] for e in ahead] + [e[3] for e in behind] + [sibling, along_z, partner] + along_x + along_y
    for target in targets:
        pl.semaphore_signal(barrier, inc=1, device_id=target, device_id_type=MESH)

    own_weights = [
        pltpu.make_async_copy(wq_hbm, wq_ref, local_sem.at[0]),
        pltpu.make_async_copy(wp_hbm, wp_ref, local_sem.at[1]),
    ]
    for copy in own_weights:
        copy.start()

    tables_ref[0] = jnp.zeros((8, 768), F32)
    tables_ref[0, :, 0:759] = table_ref[...]

    def pack(half):
        cells = []
        for ref in (tok_ref, grad_ref):
            if half == 0:
                cells.append(ref[144:432, :])
            else:
                cells.extend([ref[432:576, :], ref[0:144, :]])
        cells = jnp.concatenate(cells, axis=0)
        for di in range(2):
            packed[half, di] = jnp.dot(pack_ref[di], cells, preferred_element_type=F32).astype(BF)

    pl.semaphore_wait(barrier, len(targets))

    mine = (x * 4 + y) * 2 + core
    first = [
        send(wq_hbm.at[:, mine], other_ref.at[0:3, x, y, core], w_send.at[0], w_recv.at[0], partner),
        send(wp_hbm.at[mine], other_ref.at[3, x, y, core], w_send.at[1], w_recv.at[1], partner),
        send(tables_ref.at[0], tables_ref.at[1], w_send.at[2], w_recv.at[2], partner),
    ]
    spans = (pl.ds(0, BOTH_BIG), pl.ds(BOTH_BIG, BOTH_SMALL))
    pack(0)
    pack(1)
    pieces = []
    for n, (di, dj, to_tp, target) in enumerate(ahead):
        pieces.append(send(packed.at[to_tp, di, spans[dj]], held.at[tp, di, spans[dj]],
                           piece_send.at[n], piece_recv.at[n], target))
    own = pltpu.make_async_copy(packed.at[tp, 0, spans[0]], held.at[tp, 0, spans[0]], local_sem.at[2])
    own.start()
    pieces.append(own)

    for half in range(2):
        for c in range(4):
            for base in (288, 672):
                dparts[half, c, base:base + 96] = jnp.zeros((96, 512), BF)

    rows = lax.broadcasted_iota(jnp.int32, (WT, WT), 0) // 12
    cols = lax.broadcasted_iota(jnp.int32, (WT, WT), 1) // 12
    left = jnp.zeros((WT, WT), jnp.int32)
    right = jnp.zeros((WT, WT), jnp.int32)
    for lv in range(2):
        for row in range(6):
            value = regions_ref[row, pl.ds(2 * tp + lv, 1), 0:1]
            left = jnp.where(rows == lv * 6 + row, value, left)
            right = jnp.where(cols == lv * 6 + row, value, right)
    blocked = jnp.where(left == right, 0.0, FAR).astype(F32)

    first.pop().wait()
    blocks = []
    for s in range(2):
        table = tables_ref[s]
        top = table.astype(BF).astype(F32)
        rest = table - top
        mid = rest.astype(BF).astype(F32)
        low = rest - mid
        for part in (top, mid, low):
            for g in range(3):
                blocks.append(part[:, g * 256:(g + 1) * 256])
    matrix = jnp.concatenate(blocks, axis=0).astype(BF)
    depth = lax.broadcasted_iota(jnp.int32, (256, WT), 0)

    def some_rows(step, carry):
        found = ([], [])
        index = index_ref[pl.ds(pl.multiple_of(step * 8, 8), 8), :]
        for r in range(8):
            row = index[r:r + 1, :]
            low_part, high_part = row & 255, row >> 8
            hot = jnp.where(depth == low_part, 1.0, 0.0).astype(BF)
            picked = jnp.dot(matrix, hot, preferred_element_type=F32)
            for s in range(2):
                total = jnp.zeros((8, WT), F32)
                for g in range(3):
                    base = s * 72 + g * 8
                    value = picked[base:base + 8] + picked[base + 24:base + 32] + picked[base + 48:base + 56]
                    total = jnp.where(high_part == g, value, total)
                found[s].append(total)
        for s in range(2):
            stacked = jnp.stack(found[s], axis=0)
            bias_ref[s * 8:(s + 1) * 8, pl.ds(pl.multiple_of(step * 8, 8), 8), :] = jnp.transpose(stacked, (1, 0, 2))
        return carry

    lax.fori_loop(0, 4, some_rows, 0)
    for copy in first:
        copy.wait()

    def share(part, copies, n, target):
        copies.append(send(part, part, w_send.at[n], w_recv.at[n], target))

    third, fourth, fifth = [], [], []
    for d in range(3):
        share(other_ref.at[0:2, x, y, core], third, 3 + d, along_y[d])
        share(other_ref.at[2:4, x, y, core], third, 6 + d, along_x[d])
    lax.fori_loop(4, 10, some_rows, 0)
    lax.fori_loop(10, WT // 8, some_rows, 0)
    for h in range(16):
        bias_ref[h] = bias_ref[h] + blocked

    for copy in third + pieces:
        copy.wait()
    for d in (0, 2):
        share(other_ref.at[0:2, x, :, core], fourth, 9 + d, along_x[d])
        share(other_ref.at[2:4, :, y, core], fourth, 12 + d, along_y[d])
    share(other_ref.at[0:2, x, :, core], fifth, 15, sibling)
    share(other_ref.at[2:4, :, y, core], fifth, 16, sibling)

    def gather(which):
        halves = []
        for t in range(2):
            rows = held[t].reshape(2 * BOTH, 512)
            halves.append(jnp.dot(place_ref[which], rows, preferred_element_type=F32))
        return jnp.concatenate(halves, axis=1)

    cells = gather(0)
    center = jnp.mean(cells, axis=1, keepdims=True)
    cells = cells - center
    spread = jnp.mean(jnp.square(cells), axis=1, keepdims=True)
    inv_std = lax.rsqrt(spread + 1e-05)
    cells = cells * inv_std
    normed[...] = cells
    normed_bf[0:288] = cells.astype(BF)
    normed_bf[288:384] = jnp.zeros((96, 1024), BF)
    inv[...] = jnp.broadcast_to(inv_std, (288, 128))
    normed_t[...] = jnp.transpose(normed_bf[...], (1, 0)).reshape(32, 2, 16, 384)
    swaps = [send(normed_t.at[:, 1 - core], both_x.at[:, :, 384:768], t_send.at[1], t_recv.at[1], sibling)]
    grads[0:288] = gather(1).astype(BF)
    grads[288:384] = jnp.zeros((96, 1024), BF)
    grads_t[...] = jnp.transpose(grads[...], (1, 0)).reshape(32, 2, 16, 384)
    swaps.append(send(grads_t.at[:, 1 - core], both_g.at[:, :, 384:768], t_send.at[2], t_recv.at[2], sibling))
    both_x[:, :, 0:384] = normed_t[:, core]
    both_g[:, :, 0:384] = grads_t[:, core]

    for copy in own_weights:
        copy.wait()

    lane = lax.broadcasted_iota(jnp.int32, (WT, 128), 1)
    lower = lane < HD

    def split(value):
        zero = jnp.zeros_like(value)
        return jnp.concatenate([jnp.where(lower, value, zero), jnp.where(lower, zero, value)], axis=0)

    def weight(half, c):
        if half == 0:
            return (wq_ref[c] if c < 3 else wp_ref[...]).reshape(1024, 512)
        return other_ref[c].reshape(1024, 512)

    def project(half):
        for c in range(4):
            left = normed_bf if c < 3 else grads
            value = jnp.dot(left[0:288], weight(half, c), preferred_element_type=F32)
            value = value.astype(BF)
            if c == 0:
                value = value * jnp.asarray(0.125, BF)
            parts[c] = value

    def attend(half, start, stop):
        def pair(p, carry):
            span = pl.ds(pl.multiple_of(p * 128, 128), 128)
            for w in range(2):
                rows = pl.ds(w * WT, WT)
                q, k, v, g = (parts[c, rows, span] for c in range(4))
                qq, gg = split(q), split(g)
                bias = jnp.concatenate([bias_ref[half * 8 + 2 * p], bias_ref[half * 8 + 2 * p + 1]], axis=0)
                contract = (((1,), (1,)), ((), ()))
                flip = (((0,), (0,)), ((), ()))
                scores = lax.dot_general(qq, k, contract, preferred_element_type=F32) + bias
                weights = jnp.exp(scores)
                probs = weights / jnp.sum(weights, axis=1, keepdims=True)
                probs_bf = probs.astype(BF)
                found = jnp.dot(probs_bf, v, preferred_element_type=F32)
                dparts[half, 3, rows, span] = jnp.where(lower, found[0:WT], found[WT:]).astype(BF)
                gprobs = lax.dot_general(gg, v, contract, preferred_element_type=F32)
                dot_sum = jnp.sum(probs * gprobs, axis=1, keepdims=True)
                gscores = (probs * (gprobs - dot_sum)).astype(BF)
                gq = jnp.dot(gscores, k, preferred_element_type=F32)
                dparts[half, 0, rows, span] = (jnp.where(lower, gq[0:WT], gq[WT:]) * 0.125).astype(BF)
                dparts[half, 1, rows, span] = lax.dot_general(gscores, qq, flip, preferred_element_type=F32).astype(BF)
                dparts[half, 2, rows, span] = lax.dot_general(probs_bf, gg, flip, preferred_element_type=F32).astype(BF)
            return carry

        lax.fori_loop(start, stop, pair, 0)

    def input_grad(half):
        for c in range(3):
            value = lax.dot_general(dparts[half, c, 0:288], weight(half, c), (((1,), (1,)), ((), ())), preferred_element_type=F32)
            if half == 0 and c == 0:
                dx[...] = value
            else:
                dx[...] += value

    def swap(group, half, start, width):
        span = pl.ds(start, width)
        return send(dparts.at[half, :, 0:288, span], dparts.at[half, :, 384:672, span],
                    r_send.at[group, 0], r_recv.at[group, 0], sibling)

    def weight_grad(group, half, start, width, copy):
        mine, first_x, first_y = groups[group][0:3]
        span = pl.ds(start, width)
        copy.wait()
        stage = []
        for c in range(4):
            left = both_x if c < 3 else both_g
            value = jnp.dot(left[...].reshape(512, 768), dparts[half, c, :, span], preferred_element_type=F32)
            mine[c] = value.astype(BF).reshape(4, 2, 4, 16, width)
            for d in range(3):
                n = 1 + 3 * c + d
                if c % 2 == 0:
                    stage.append(send(mine.at[c, (x + d + 1) % 4], first_x.at[c // 2, d],
                                      r_send.at[group, n], r_recv.at[group, n], along_x[d]))
                else:
                    stage.append(send(mine.at[c, :, :, (y + d + 1) % 4], first_y.at[c // 2, d],
                                      r_send.at[group, n], r_recv.at[group, n], along_y[d]))
        return stage

    def plus(value, others):
        value = value.astype(F32)
        for d in range(3):
            value += others[d].astype(F32)
        return value

    def reduce_second(group, copies):
        mine, first_x, first_y, mid_x, mid_y, second_x, second_y = groups[group][0:7]
        for copy in copies:
            copy.wait()
        for n in range(2):
            mid_x[n] = plus(mine[2 * n, x], first_x[n]).astype(BF)
            mid_y[n] = plus(mine[2 * n + 1, :, :, y], first_y[n]).astype(BF)
        stage = []
        for d in range(3):
            stage.append(send(mid_x.at[:, :, (y + d + 1) % 4], second_x.at[d],
                              r_send.at[group, 13 + d], r_recv.at[group, 13 + d], along_y[d]))
            stage.append(send(mid_y.at[:, (x + d + 1) % 4], second_y.at[d],
                              r_send.at[group, 16 + d], r_recv.at[group, 16 + d], along_x[d]))
        return stage

    def reduce_third(group, copies):
        mid_x, mid_y, second_x, second_y, z_out, z_in = groups[group][3:9]
        for copy in copies:
            copy.wait()
        for n in range(2):
            z_out[2 * n] = plus(mid_x[n, :, y], [second_x[d, n] for d in range(3)]).astype(BF)
            z_out[2 * n + 1] = plus(mid_y[n, x], [second_y[d, n] for d in range(3)]).astype(BF)
        return [
            send(z_out.at[:, zl], z_in.at[0], r_send.at[group, 19], r_recv.at[group, 19], partner),
            send(z_out.at[:, 1 - zl], z_in.at[1], r_send.at[group, 20], r_recv.at[group, 20], diagonal),
        ]

    def early_grad(group, half, start, width, copy):
        mine, first_x, first_y, first_z = groups[group][0:4]
        span = pl.ds(start, width)
        copy.wait()
        stage = []
        for c in (2, 3, 0, 1):
            left = both_x if c < 3 else both_g
            value = jnp.dot(left[...].reshape(512, 768), dparts[half, c, :, span], preferred_element_type=F32)
            mine[c] = value.astype(BF).reshape(4, 2, 4, 16, width)
            if c == 3:
                stage.append(send(mine.at[2:4, :, 1 - zl], first_z, r_send.at[group, 1], r_recv.at[group, 1], along_z))
            for d in range(3):
                if c == 0:
                    stage.append(send(mine.at[0, (x + d + 1) % 4], first_x.at[d],
                                      r_send.at[group, 2 + d], r_recv.at[group, 2 + d], along_x[d]))
                if c == 1:
                    stage.append(send(mine.at[1, :, :, (y + d + 1) % 4], first_y.at[d],
                                      r_send.at[group, 5 + d], r_recv.at[group, 5 + d], along_y[d]))
        return stage

    def early_second(group, copies):
        mine, first_x, first_y, first_z, mid_x, mid_y, mid_z, second_x, second_y, second_zx, second_zy = groups[group][0:11]
        for copy in copies:
            copy.wait()
        mid_x[...] = plus(mine[0, x], first_x).astype(BF)
        mid_y[...] = plus(mine[1, :, :, y], first_y).astype(BF)
        mid_z[...] = (mine[2:4, :, zl].astype(F32) + first_z[...].astype(F32)).astype(BF)
        stage = []
        for d in range(3):
            to_x, to_y = (x + d + 1) % 4, (y + d + 1) % 4
            for n, (src, dst, target) in enumerate((
                (mid_z.at[0, to_x], second_zx.at[d], along_x[d]),
                (mid_z.at[1, :, to_y], second_zy.at[d], along_y[d]),
                (mid_x.at[:, to_y], second_x.at[d], along_y[d]),
                (mid_y.at[to_x], second_y.at[d], along_x[d]),
            )):
                stage.append(send(src, dst, r_send.at[group, 8 + 4 * d + n], r_recv.at[group, 8 + 4 * d + n], target))
        return stage

    def early_third(group, copies):
        (mid_x, mid_y, mid_z, second_x, second_y, second_zx, second_zy, z_out, z_in,
         late_x, late_y, third_x, third_y) = groups[group][4:17]
        for copy in copies:
            copy.wait()
        z_out[0] = plus(mid_x[:, y], second_x).astype(BF)
        z_out[1] = plus(mid_y[x], second_y).astype(BF)
        late_x[...] = plus(mid_z[0, x], second_zx).astype(BF)
        late_y[...] = plus(mid_z[1, :, y], second_zy).astype(BF)
        stage = [send(z_out.at[:, 1 - zl], z_in, r_send.at[group, 20], r_recv.at[group, 20], along_z)]
        for d in range(3):
            stage.append(send(late_x.at[(y + d + 1) % 4], third_x.at[d],
                              r_send.at[group, 21 + d], r_recv.at[group, 21 + d], along_y[d]))
            stage.append(send(late_y.at[(x + d + 1) % 4], third_y.at[d],
                              r_send.at[group, 24 + d], r_recv.at[group, 24 + d], along_x[d]))
        return stage

    def early_last(group, copies):
        z_out, z_in, late_x, late_y, third_x, third_y, done = groups[group][11:18]
        for copy in copies:
            copy.wait()
        for c in range(2):
            done[c] = z_out[c, zl].astype(F32) + z_in[c].astype(F32)
        done[2] = plus(late_x[y], third_x)
        done[3] = plus(late_y[x], third_y)

    project(0)
    attend(0, 0, 2)
    for copy in fourth:
        copy.wait()
    relay = []
    for d in (0, 2):
        from_y, from_x = (y + 3 - d) % 4, (x + 3 - d) % 4
        part = pl.ds(d, 2)
        share(other_ref.at[0:2, from_x, part, core], relay, 23 + d, along_x[d])
        share(other_ref.at[2:4, part, from_y, core], relay, 24 + d, along_y[d])
        share(other_ref.at[0:2, from_x, :, core], fifth, 17 + d, sibling)
        share(other_ref.at[2:4, :, from_y, core], fifth, 20 + d, sibling)
    attend(0, 2, 4)
    step = swap(0, 0, 0, 512)
    input_grad(0)
    for copy in swaps + relay:
        copy.wait()
    share(other_ref.at[0:2, (x + 2) % 4, :, core], fifth, 18, sibling)
    share(other_ref.at[2:4, :, (y + 2) % 4, core], fifth, 21, sibling)
    stage0 = early_grad(0, 0, 0, 512, step)
    for copy in fifth:
        copy.wait()
    project(1)
    attend(1, 0, 2)
    step = swap(1, 1, 0, 256)
    attend(1, 2, 3)
    stage1 = weight_grad(1, 1, 0, 256, step)
    attend(1, 3, 4)
    step = swap(2, 1, 256, 256)
    input_grad(1)
    stage2 = weight_grad(2, 1, 256, 256, step)
    stage0 = early_second(0, stage0)

    total = dx[...]
    mean_grad = jnp.mean(total, axis=1, keepdims=True)
    mean_cross = jnp.mean(total * normed[...], axis=1, keepdims=True)
    result = (inv[:, 0:1] * (total - mean_grad - normed[...] * mean_cross)).astype(BF)
    moved = jnp.dot(placet_ref[...], result, preferred_element_type=F32).astype(BF)
    for di in range(2):
        for t in range(2):
            back[t, di] = moved[di * PIECE:(di + 1) * PIECE, t * 512:(t + 1) * 512]

    spans = (pl.ds(0, BIG), pl.ds(BIG, SMALL))
    pieces = []
    for n, (di, dj, to_tp, target) in enumerate(behind):
        pieces.append(send(back.at[to_tp, di, spans[dj]], landed.at[tp, di, spans[dj]],
                           back_send.at[n], back_recv.at[n], target))
    own = pltpu.make_async_copy(back.at[tp, 0, spans[0]], landed.at[tp, 0, spans[0]], local_sem.at[3])
    own.start()
    pieces.append(own)
    stage1 = reduce_second(1, stage1)
    stage2 = reduce_second(2, stage2)
    stage0 = early_third(0, stage0)
    stage1 = reduce_third(1, stage1)
    stage2 = reduce_third(2, stage2)
    early_last(0, stage0)
    for copy in pieces + stage1 + stage2:
        copy.wait()
    done = groups[0][17]
    for group, span in ((1, pl.ds(0, 256)), (2, pl.ds(256, 256))):
        others = groups[group][8]
        total_ref[:, :, span] = (done[:, :, span] + others[0].astype(F32) + others[1].astype(F32))


def early_scratch(width):
    shapes = ((4, 4, 2, 4), (3, 2, 4), (3, 4, 2), (2, 4, 4), (2, 4), (4, 2), (2, 4, 4),
              (3, 2), (3, 2), (3, 4), (3, 4), (2, 2), (2,), (4,), (4,), (3,), (3,))
    return [pltpu.VMEM(shape + (16, width), BF) for shape in shapes] + [pltpu.VMEM((4, 16, width), F32)]


def group_scratch(width):
    shapes = ((4, 4, 2, 4), (2, 3, 2, 4), (2, 3, 4, 2), (2, 2, 4), (2, 4, 2), (3, 2, 2), (3, 2, 2), (4, 2), (2, 4))
    return [pltpu.VMEM(shape + (16, width), BF) for shape in shapes]


def finish_kernel(landed, total_ref, packt_ref, tokens_ref, qkv_ref, proj_ref):
    for t in range(2):
        cells = landed[t].reshape(2 * PIECE, 512)
        moved = jnp.dot(packt_ref[...], cells, preferred_element_type=F32).astype(BF)
        if t == 0:
            tokens_ref[144:432, :] = moved
        else:
            tokens_ref[432:576, :] = moved[0:144]
            tokens_ref[0:144, :] = moved[144:288]
    qkv_ref[...] = total_ref[0:3]
    proj_ref[...] = total_ref[3]


VM = pl.BlockSpec(memory_space=pltpu.VMEM)
HB = pl.BlockSpec(memory_space=pl.ANY)
LIMIT = 60 * 1024 * 1024


def shards(tokens, w_qkv, w_proj, bias_table, bias_index, regions, out_grad):
    flat_in = tokens.reshape(576, 512)
    flat_grad = out_grad.reshape(576, 512)
    wq = w_qkv.transpose(1, 0, 2).reshape(3, 32, 32, 512)
    wp = w_proj.reshape(32, 32, 512)
    pack = jnp.asarray(PACK, BF)
    packt = jnp.asarray(UNPACK, BF)
    place = jnp.asarray(PLACE, BF)
    placet = jnp.asarray(LEAVE, BF)
    dma = pltpu.SemaphoreType.DMA
    shape = jax.ShapeDtypeStruct
    vmem = pltpu.VMEM
    landed, total = pl.pallas_call(
        whole_kernel,
        out_shape=(shape((2, 2, PIECE, 512), BF), shape((4, 16, 512), F32)),
        in_specs=[VM] * 5 + [HB] * 2 + [VM] * 3,
        out_specs=(VM, VM),
        scratch_shapes=[
            vmem((3, 32, 32, 512), BF), vmem((32, 32, 512), BF),
            vmem((4, 4, 4, 2, 32, 512), BF), vmem((2, 8, 768), F32),
            vmem((2, 2, BOTH, 512), BF), vmem((2, 2, BOTH, 512), BF), vmem((16, WT, WT), F32),
            vmem((288, 1024), F32), vmem((384, 1024), BF), vmem((384, 1024), BF),
            vmem((32, 2, 16, 384), BF), vmem((32, 2, 16, 384), BF), vmem((32, 16, 768), BF), vmem((32, 16, 768), BF),
            vmem((288, 128), F32), vmem((4, 288, 512), BF), vmem((2, 4, 768, 512), BF),
            vmem((288, 1024), F32), vmem((2, 2, PIECE, 512), BF),
            *early_scratch(512), *group_scratch(256), *group_scratch(256),
            dma((7,)), dma((7,)), dma((7,)), dma((7,)), dma((27,)), dma((27,)), dma((3, 27)), dma((3, 27)), dma((3,)), dma((3,)), dma((4,)),
        ],
        compiler_params=pltpu.CompilerParams(collective_id=0, has_side_effects=True, vmem_limit_bytes=LIMIT),
        name="whole",
    )(flat_in, flat_grad, pack, place, placet, wq, wp, bias_table.T, bias_index, regions.transpose(1, 0, 2))

    grad_tokens, qkv_grad, proj_grad = pl.pallas_call(
        finish_kernel,
        out_shape=(shape((576, 512), BF), shape((3, 16, 512), F32), shape((16, 512), F32)),
        in_specs=[VM] * 3,
        out_specs=(VM, VM, VM),
        name="finish",
    )(landed, total, packt)
    return grad_tokens.reshape(tokens.shape), qkv_grad.transpose(1, 0, 2), proj_grad


def solution(mesh):
    in_specs = (
        P(None, "lat", "lon", "tp"),
        P(None, None, "tp"),
        P(None, "tp"),
        P(None, "tp"),
        P(),
        P(None, "lat", "lon"),
        P(None, "lat", "lon", "tp"),
    )
    out_specs = (
        P(None, "lat", "lon", "tp"),
        P(("lat", "lon"), None, "tp"),
        P(("lat", "lon"), "tp"),
    )
    return jax.shard_map(shards, mesh=mesh, in_specs=in_specs, out_specs=out_specs, check_vma=False)
```
